256 devices in a mesh: dp: 32 (over x, z), tensor: 8 (over y, core).
Axes of the slice: x: 4, y: 4, z: 8, core: 2. Of those that a mesh axis runs over, the one named last changes fastest.
Arguments:
- queries: bfloat16 [3072, 3, 4096], P('dp', None, 'tensor'), may hold values from -600 to 600
- prompt_cache: bfloat16 [64, 2, 4096, 1024], P('dp', None, None, 'tensor'), may hold values from -6 to 6
- tails: bfloat16 [3072, 2, 64, 1024], P('dp', None, None, 'tensor'), may hold values from -5 to 5
- fresh: bfloat16 [3072, 3, 2, 1024], P('dp', None, None, 'tensor'), may hold values from -5 to 5
- residual: bfloat16 [3072, 3, 4096], P('dp', None, 'tensor'), may hold values from -6 to 6
- out_proj: bfloat16 [4096, 4096], P('tensor'), may hold values from -0.75 to 0.75
- lengths: int32 [3072], P('dp'), may hold values from 1 to 61, as said below
- prompt_of: int32 [3072], P('dp'), may hold values from 0 to 63, as said below
- moves: int32 [496, 3], replicated, may hold values from 0 to 3071, as said below
Outputs:
- mixed: bfloat16 [4064, 3, 4096], P('dp', None, 'tensor')
- tails_out: bfloat16 [4064, 2, 64, 1024], P('dp', None, None, 'tensor')
The draws below stay inside these ranges and needn't reach their ends.
Inputs may be any that keep to these rules, and one draw needn't show every extreme that they name: `lengths`: on every dp index some branch has exactly 61. `prompt_of`: branch b's prompt is one of the 2 prompts held by the same dp index: from (b // 96) * 2 to that plus 2 - 1. `moves`: column 0 is a branch, column 1 the dp index that holds it, column 2 another dp index. Half of the dp indices send and the other half receive; every sender sends exactly 31 branches and every receiver receives exactly 31; every sender sends two branches to every receiver but one and one branch to that one; no branch is listed twice.
All inputs are finite; a program needn't handle non-finite values.
Results may differ from the reference program's by a relative error of at most 0.018.
Values may be sent and summed in bfloat16 or wider, within the bound.
A program may use at most 128 MiB of HBM per device.

```python
import math
import jax
import jax.numpy as jnp
from jax import lax

WIDTH = 4096
HEADS = 32
KV_HEADS = 8
HEAD = 128
PROMPT = 4096
NEW = 3
PR_DEV = 2
TAIL = 64
B_DEV = 96
MOVES = 496
SLOTS = 127
BRANCHES = 3072
PROMPTS = 64
N_DP = 32
N_TENSOR = 8


def draw_queries(key, part):
    key = jax.random.fold_in(key, 1)
    values_drawn = jnp.clip(jax.random.normal(key, (BRANCHES, NEW, HEADS * HEAD)), -5.0, 5.0)
    return values_drawn.astype(jnp.bfloat16)


def draw_tails(key, part):
    key = jax.random.fold_in(key, 2)
    values_drawn = jnp.clip(jax.random.normal(key, (BRANCHES, 2, TAIL, KV_HEADS * HEAD)), -5.0, 5.0)
    return values_drawn.astype(jnp.bfloat16)


def draw_fresh(key, part):
    key = jax.random.fold_in(key, 3)
    values_drawn = jnp.clip(jax.random.normal(key, (BRANCHES, NEW, 2, KV_HEADS * HEAD)), -5.0, 5.0)
    return values_drawn.astype(jnp.bfloat16)


def draw_lengths(key, part):
    key = jax.random.fold_in(key, 21)
    lengths_drawn = jax.random.randint(jax.random.fold_in(key, 1), (BRANCHES,), 1, TAIL - NEW + 1)
    longest = jax.random.randint(jax.random.fold_in(key, 2), (N_DP,), 0, B_DEV) + jnp.arange(N_DP, dtype=jnp.int32) * B_DEV
    marked = jnp.repeat(longest, B_DEV) == jnp.arange(BRANCHES, dtype=jnp.int32)
    return jnp.where(marked, TAIL - NEW, lengths_drawn).astype(jnp.int32)


def draw_prompt_of(key, part):
    key = jax.random.fold_in(key, 31)
    offsets = jax.random.randint(key, (BRANCHES,), 0, PR_DEV)
    return (jnp.arange(BRANCHES, dtype=jnp.int32) // B_DEV * PR_DEV + offsets).astype(jnp.int32)


def draw_moves(key, part):
    key = jax.random.fold_in(key, 41)
    halfway = N_DP // 2
    doubled = halfway - 1
    others = jax.random.permutation(jax.random.fold_in(key, 1), N_DP - 1).astype(jnp.int32)
    senders = jnp.concatenate([jnp.full((1,), N_DP - 1, jnp.int32), others[:halfway - 1]])
    takers = others[halfway - 1:]
    sender_ids = jnp.arange(halfway, dtype=jnp.int32)
    counts = 1 + ((sender_ids[None, :] - sender_ids[:, None]) % halfway < doubled).astype(jnp.int32)
    repeat_index = jnp.arange(2, dtype=jnp.int32)
    usable = repeat_index[None, None, :] < counts[:, :, None]
    ordinal = jnp.cumsum(usable.reshape(halfway, 2 * halfway).astype(jnp.int32), axis=1) - 1
    ranking = jax.random.randint(jax.random.fold_in(key, 2), (halfway, B_DEV), 0, 1 << 20) * B_DEV
    ranking = ranking + jnp.arange(B_DEV, dtype=jnp.int32)[None, :]
    ranking = ranking.at[0, B_DEV - 1].set(-1)
    slot_order = jnp.argsort(ranking, axis=1, stable=True).astype(jnp.int32)
    chosen_slot = jnp.take_along_axis(slot_order, jnp.clip(ordinal, 0, B_DEV - 1), axis=1)
    source_flat = jnp.broadcast_to(senders[:, None], (halfway, 2 * halfway)).reshape(-1)
    target_flat = jnp.broadcast_to(takers[None, :, None], (halfway, halfway, 2)).reshape(-1)
    branch_flat = source_flat * B_DEV + chosen_slot.reshape(-1)
    usable_flat = usable.reshape(-1).astype(jnp.int32)
    mixing = jax.random.permutation(jax.random.fold_in(key, 3), 2 * halfway * halfway).astype(jnp.int32)
    sorted_order = mixing[jnp.argsort(1 - usable_flat[mixing], stable=True)]
    chosen_entries = sorted_order[:MOVES]
    listed = jnp.stack([branch_flat[chosen_entries], source_flat[chosen_entries], target_flat[chosen_entries]], axis=1)
    return listed.astype(jnp.int32)


def raised(drawn, own_key, source, target, blocks, factor):
    def block_of(axis_at):
        return (jnp.arange(drawn.shape[axis_at]) // (drawn.shape[axis_at] // blocks)).reshape((-1,) + (1,) * (drawn.ndim - 1 - axis_at))

    one_side = jax.random.permutation(own_key, blocks)[block_of(target)]
    other_side = (block_of(target) + blocks // 2) % blocks
    return jnp.where((block_of(source) == one_side) | (block_of(source) == other_side), factor * drawn, drawn)


def level_of(rng, shape, cuts, smallest, high):
    gain = 1.0
    for position, shards_of in cuts:
        heights = jax.random.uniform(jax.random.fold_in(jax.random.fold_in(rng, 6), position), (shards_of,), jnp.float32, smallest / len(cuts), high / len(cuts))
        gain = gain * jnp.repeat(jnp.exp(heights), shape[position] // shards_of).reshape((-1,) + (1,) * (len(shape) - 1 - position))
    return gain


def normal_values(key, dims, deviation, most, pieces=(), held_as=jnp.bfloat16):
    values = deviation * jax.random.normal(key, dims, jnp.float32)
    if pieces:
        values = values * level_of(key, dims, pieces, -0.22, 0.18)
    return jnp.clip(values, -most, most).astype(held_as)


def heavy_noise(rng, dims, spread, limit, pieces, heavy, held_as=jnp.bfloat16):
    array = spread * jax.random.normal(rng, dims, jnp.float32)
    if pieces:
        array = array * level_of(rng, dims, pieces, -0.22, 0.18)
    return jnp.clip(raised(array, jax.random.fold_in(rng, 3), *heavy), -limit, limit).astype(held_as)


def setup_inputs(seed: int = 0) -> dict:
    streams_of = jax.random.split(jax.random.key(seed), 10)
    queries = draw_queries(jax.random.fold_in(streams_of[9], 71), 0)
    prompt_cache = normal_values(streams_of[1], (PROMPTS, 2, PROMPT, KV_HEADS * HEAD), 1.0, 6.0, ((0, 32), (3, 8)))
    tails = draw_tails(jax.random.fold_in(streams_of[9], 71), 0)
    fresh = draw_fresh(jax.random.fold_in(streams_of[9], 71), 0)
    residual = normal_values(streams_of[4], (BRANCHES, NEW, WIDTH), 1.0, 6.0, ((0, 32), (2, 8)))
    out_proj = heavy_noise(streams_of[5], (HEADS * HEAD, WIDTH), HEAD ** -0.5, 0.75, ((0, 8),), (0, 1, 8, 2.0))
    lengths = draw_lengths(jax.random.fold_in(streams_of[9], 71), 0)
    prompt_of = draw_prompt_of(jax.random.fold_in(streams_of[9], 71), 0)
    moves = draw_moves(jax.random.fold_in(streams_of[9], 71), 0)
    return {"queries": queries, "prompt_cache": prompt_cache, "tails": tails, "fresh": fresh, "residual": residual, "out_proj": out_proj, "lengths": lengths, "prompt_of": prompt_of, "moves": moves}


def attend_group(inputs):
    queries_here, cache_here, local_prompt, tails_here, fresh_here, lengths_here = inputs
    branches_here = queries_here.shape[0]
    share = HEADS // KV_HEADS
    scale = 1.0 / math.sqrt(HEAD)
    grouped = queries_here.astype(jnp.float32).reshape(branches_here, NEW, KV_HEADS, share, HEAD)
    prefix = None
    for prompt_index in range(PR_DEV):
        keys_here = cache_here[prompt_index, 0].astype(jnp.float32).reshape(PROMPT, KV_HEADS, HEAD)
        scores = jnp.einsum('bnkgd,tkd->bnkgt', grouped, keys_here) * scale
        chosen = (local_prompt == prompt_index)[:, None, None, None, None]
        picked = jnp.where(chosen, scores, 0.0)
        prefix = picked if prefix is None else prefix + picked
    tail_keys = tails_here[:, 0].astype(jnp.float32).reshape(branches_here, TAIL, KV_HEADS, HEAD)
    tail_scores = jnp.einsum('bnkgd,btkd->bnkgt', grouped, tail_keys) * scale
    fresh_keys = fresh_here[:, :, 0].astype(jnp.float32).reshape(branches_here, NEW, KV_HEADS, HEAD)
    fresh_scores = jnp.einsum('bnkgd,bmkd->bnkgm', grouped, fresh_keys) * scale
    tail_visible = (jnp.arange(TAIL, dtype=jnp.int32)[None, :] < lengths_here[:, None])[:, None, None, None, :]
    fresh_visible = (jnp.arange(NEW, dtype=jnp.int32)[None, :] <= jnp.arange(NEW, dtype=jnp.int32)[:, None])[None, :, None, None, :]
    row_max = lax.optimization_barrier(jnp.max(prefix, axis=-1, keepdims=True))
    row_max = jnp.maximum(row_max, lax.optimization_barrier(jnp.max(jnp.where(tail_visible, tail_scores, -jnp.inf), axis=-1, keepdims=True)))
    row_max = jnp.maximum(row_max, lax.optimization_barrier(jnp.max(jnp.where(fresh_visible, fresh_scores, -jnp.inf), axis=-1, keepdims=True)))
    prefix_expo = jnp.exp(prefix - row_max)
    tail_expo = jnp.where(tail_visible, jnp.exp(tail_scores - row_max), 0.0)
    fresh_expo = jnp.where(fresh_visible, jnp.exp(fresh_scores - row_max), 0.0)
    denominator = lax.optimization_barrier(jnp.sum(prefix_expo, -1)) + lax.optimization_barrier(jnp.sum(tail_expo, -1)) + lax.optimization_barrier(jnp.sum(fresh_expo, -1))
    prefix_weights = lax.optimization_barrier(prefix_expo.astype(jnp.bfloat16)).astype(jnp.float32)
    tail_weights = lax.optimization_barrier(tail_expo.astype(jnp.bfloat16)).astype(jnp.float32)
    fresh_weights = lax.optimization_barrier(fresh_expo.astype(jnp.bfloat16)).astype(jnp.float32)
    accumulated = jnp.zeros((branches_here, NEW, KV_HEADS, share, HEAD), jnp.float32)
    for prompt_index in range(PR_DEV):
        values_here = cache_here[prompt_index, 1].astype(jnp.float32).reshape(PROMPT, KV_HEADS, HEAD)
        chosen = (local_prompt == prompt_index)[:, None, None, None, None]
        accumulated = accumulated + jnp.einsum('bnkgt,tkd->bnkgd', jnp.where(chosen, prefix_weights, 0.0), values_here)
    tail_values = tails_here[:, 1].astype(jnp.float32).reshape(branches_here, TAIL, KV_HEADS, HEAD)
    accumulated = accumulated + jnp.einsum('bnkgt,btkd->bnkgd', tail_weights, tail_values)
    fresh_values = fresh_here[:, :, 1].astype(jnp.float32).reshape(branches_here, NEW, KV_HEADS, HEAD)
    accumulated = accumulated + jnp.einsum('bnkgm,bmkd->bnkgd', fresh_weights, fresh_values)
    result = accumulated / denominator[..., None]
    return result.astype(jnp.bfloat16).reshape(branches_here, NEW, HEADS * HEAD)

def write_tail(tail_here, fresh_here, length_here):
    rows = jnp.transpose(fresh_here, (1, 0, 2))
    zero_index = jnp.zeros((), jnp.int32)
    return lax.dynamic_update_slice(tail_here, rows, (zero_index, length_here, zero_index))

def reference(queries, prompt_cache, tails, fresh, residual, out_proj, lengths, prompt_of, moves):
    branch_index = jnp.arange(BRANCHES, dtype=jnp.int32)
    local_prompt = prompt_of - branch_index // B_DEV * PR_DEV
    grouped_inputs = (queries.reshape(N_DP, B_DEV, NEW, HEADS * HEAD), prompt_cache.reshape(N_DP, PR_DEV, 2, PROMPT, KV_HEADS * HEAD), local_prompt.reshape(N_DP, B_DEV), tails.reshape(N_DP, B_DEV, 2, TAIL, KV_HEADS * HEAD), fresh.reshape(N_DP, B_DEV, NEW, 2, KV_HEADS * HEAD), lengths.reshape(N_DP, B_DEV))
    heads_out = lax.map(attend_group, grouped_inputs).reshape(BRANCHES * NEW, HEADS * HEAD)
    block = HEADS * HEAD // N_TENSOR
    summed = jnp.zeros((BRANCHES * NEW, WIDTH), jnp.float32)
    for block_index in range(N_TENSOR):
        partial_value = jnp.dot(heads_out[:, block_index * block:(block_index + 1) * block], out_proj[block_index * block:(block_index + 1) * block], preferred_element_type=jnp.float32)
        partial_value = lax.optimization_barrier(partial_value.astype(jnp.bfloat16)).astype(jnp.float32)
        summed = summed + partial_value
    mixed_rows = (residual.reshape(BRANCHES * NEW, WIDTH).astype(jnp.float32) + summed).astype(jnp.bfloat16)
    mixed_rows = mixed_rows.reshape(BRANCHES, NEW, WIDTH)
    tails_written = jax.vmap(write_tail)(tails, fresh, lengths)
    entries = jnp.arange(MOVES, dtype=jnp.int32)
    target = moves[:, 2]
    earlier = (entries[None, :] < entries[:, None]) & (target[None, :] == target[:, None])
    arrival = lax.optimization_barrier(jnp.sum(earlier.astype(jnp.int32), axis=1))
    home_slot = branch_index // B_DEV * SLOTS + branch_index % B_DEV
    slot = home_slot.at[moves[:, 0]].set(target * SLOTS + B_DEV + arrival)
    mixed = jnp.zeros((N_DP * SLOTS, NEW, WIDTH), jnp.bfloat16).at[slot].set(mixed_rows)
    tails_out = jnp.zeros((N_DP * SLOTS, 2, TAIL, KV_HEADS * HEAD), jnp.bfloat16).at[slot].set(tails_written)
    return (mixed, tails_out)
```

```python
import math

import jax
import jax.numpy as jnp
from jax import lax
from jax.experimental import pallas as pl
from jax.experimental.pallas import tpu as pltpu
from jax.sharding import PartitionSpec as P

HEAD = 128
GROUP = 16
TILES = 2
CHUNK = 512
CORES = 2
ROW = 16
MIB = 1 << 20
MESH = pl.DeviceIdType.MESH


def written_rows(rows, fresh, length):
    at = lax.broadcasted_iota(jnp.int32, rows.shape, 0)
    wide = rows.astype(jnp.float32)
    for i, line in enumerate(fresh):
        wide = jnp.where(at == length + i, line, wide)
    return wide.astype(rows.dtype)


def fresh_of(fresh_ref, branch, kind):
    pairs = [fresh_ref[branch, i].astype(jnp.float32) for i in range(fresh_ref.shape[1])]
    return [pair[kind : kind + 1] for pair in pairs]


def attend_tile(first, query_ref, cache, tails, fresh_wide, length_ref, second_ref, heads, scores):
    new_count = query_ref.shape[0]
    share = query_ref.shape[2] // HEAD
    keys = cache.shape[2]
    tail_rows = tails.shape[2]
    tail_keys = GROUP * tail_rows
    blocks = new_count * share
    rows = blocks * GROUP
    factor = math.log2(math.e) / math.sqrt(HEAD)
    contract_last = (((1,), (1,)), ((), ()))

    def lanes(op, value, carry):
        for at in range(0, value.shape[1], HEAD):
            carry = op(carry, value[:, at : at + HEAD])
        return carry

    def fresh_block(kind):
        parts = [fresh_wide[kind, i, pl.ds(first, GROUP)] for i in range(new_count)]
        parts.append(jnp.zeros((HEAD - new_count * GROUP, HEAD), jnp.float32))
        return jnp.concatenate(parts, axis=0).astype(jnp.bfloat16)

    query = jnp.concatenate(
        [
            query_ref[i, pl.ds(first, GROUP), h * HEAD : (h + 1) * HEAD]
            for i in range(new_count)
            for h in range(share)
        ],
        axis=0,
    )
    second = jnp.concatenate([second_ref[pl.ds(first, GROUP)]] * blocks, axis=0) > 0
    nothing = jnp.zeros_like(query)
    both = jnp.concatenate(
        [jnp.where(second, nothing, query), jnp.where(second, query, nothing)], axis=1
    )
    top = jnp.full((rows, HEAD), -jnp.inf, jnp.float32)
    for at in range(0, keys, CHUNK):
        key_block = jnp.concatenate(
            [cache[0, 0, at : at + CHUNK], cache[1, 0, at : at + CHUNK]], axis=1
        )
        block = lax.dot_general(both, key_block, contract_last, preferred_element_type=jnp.float32)
        scores[:, at : at + CHUNK] = block
        top = lanes(jnp.maximum, block, top)
    tail_scores = lax.dot_general(
        query,
        tails[pl.ds(first, GROUP), 0].reshape(tail_keys, HEAD),
        contract_last,
        preferred_element_type=jnp.float32,
    )
    length = jnp.concatenate([length_ref[pl.ds(first, GROUP)]] * blocks, axis=0)
    row_at = lax.broadcasted_iota(jnp.int32, (rows, HEAD), 0)
    key_at = lax.broadcasted_iota(jnp.int32, (rows, HEAD), 1)
    held = []
    for at in range(0, tail_keys, HEAD):
        seen = (row_at % GROUP == (key_at + at) // tail_rows) & (key_at % tail_rows < length)
        held.append(jnp.where(seen, tail_scores[:, at : at + HEAD], -jnp.inf))
    tail_scores = jnp.concatenate(held, axis=1)
    fresh_scores = lax.dot_general(
        query, fresh_block(0), contract_last, preferred_element_type=jnp.float32
    )
    seen = (row_at % GROUP == key_at % GROUP) & (key_at // GROUP <= row_at // (GROUP * share))
    fresh_scores = jnp.where(seen, fresh_scores, -jnp.inf)
    top = jnp.maximum(lanes(jnp.maximum, tail_scores, top), fresh_scores)
    top = jnp.max(top, axis=1, keepdims=True)
    total = jnp.zeros((rows, HEAD), jnp.float32)
    pair = jnp.zeros((rows, 2 * HEAD), jnp.float32)
    for at in range(0, keys, CHUNK):
        expo = jnp.exp2((scores[:, at : at + CHUNK] - top) * factor)
        total = lanes(jnp.add, expo, total)
        value_block = jnp.concatenate(
            [cache[0, 1, at : at + CHUNK], cache[1, 1, at : at + CHUNK]], axis=1
        )
        pair += jnp.dot(expo.astype(jnp.bfloat16), value_block, preferred_element_type=jnp.float32)
    mixed = jnp.where(second, pair[:, HEAD:], pair[:, :HEAD])
    expo = jnp.exp2((tail_scores - top) * factor)
    total = lanes(jnp.add, expo, total)
    mixed += jnp.dot(
        expo.astype(jnp.bfloat16),
        tails[pl.ds(first, GROUP), 1].reshape(tail_keys, HEAD),
        preferred_element_type=jnp.float32,
    )
    expo = jnp.exp2((fresh_scores - top) * factor)
    total += expo
    mixed += jnp.dot(
        expo.astype(jnp.bfloat16), fresh_block(1), preferred_element_type=jnp.float32
    )
    result = (mixed / jnp.sum(total, axis=1, keepdims=True)).astype(heads.dtype)
    for i in range(new_count):
        for h in range(share):
            at = (i * share + h) * GROUP
            heads[i, pl.ds(first, GROUP), h * HEAD : (h + 1) * HEAD] = result[at : at + GROUP]


def block_kernel(
    groups,
    chips,
    take_ref,
    branch_length_ref,
    stay_ref,
    query_ref,
    residual_ref,
    fresh_ref,
    length_ref,
    second_ref,
    tails_in,
    cache_in,
    proj_in,
    rows_out,
    arrived_rows,
    arrived_tails,
    home_out,
    tails,
    cache,
    proj,
    staged,
    staged_rows,
    fresh_wide,
    scores,
    heads,
    own,
    pair_send,
    pair_recv,
    chip_send,
    chip_recv,
    wide_rows,
    load_sems,
    tail_send_sems,
    tail_recv_sems,
    row_send_sems,
    row_recv_sems,
    pair_send_sems,
    pair_recv_sems,
    chip_send_sems,
    chip_recv_sems,
):
    new_count, branches_here, width = query_ref.shape
    me = lax.axis_index("dp")
    place = lax.axis_index("tensor")
    chip, core = place // CORES, place % CORES
    other = chip * CORES + (CORES - 1 - core)
    spans = GROUP * TILES
    chunks = branches_here // spans

    def peer_of(step):
        return lax.rem(me + step, groups)

    def chip_of(step):
        return lax.rem(chip + step, chips)

    barrier = pltpu.get_barrier_semaphore()

    def greet(step, carry):
        pl.semaphore_signal(
            barrier, inc=1, device_id=(peer_of(step), place), device_id_type=MESH
        )
        return carry

    load_tails = pltpu.make_async_copy(tails_in, tails, load_sems.at[0])
    load_cache = pltpu.make_async_copy(cache_in, cache, load_sems.at[1])
    load_proj = pltpu.make_async_copy(proj_in, proj, load_sems.at[2])
    load_tails.start()
    load_cache.start()
    load_proj.start()
    lax.fori_loop(1, groups, greet, 0)
    pl.semaphore_signal(barrier, inc=1, device_id=(me, other), device_id_type=MESH)
    for step in range(1, chips):
        pl.semaphore_signal(
            barrier,
            inc=1,
            device_id=(me, chip_of(step) * CORES + core),
            device_id_type=MESH,
        )

    load_tails.wait()

    def pack(slot, carry):
        branch = take_ref[slot]
        length = branch_length_ref[branch]
        for kind in range(2):
            staged[slot // 2, slot % 2, kind] = written_rows(
                tails[branch, kind], fresh_of(fresh_ref, branch, kind), length
            )
        return carry

    lax.fori_loop(0, groups * 2, pack, 0)
    pl.semaphore_wait(barrier, groups - 1 + 1 + chips - 1)

    def tail_copy(step):
        return pltpu.make_async_remote_copy(
            src_ref=staged.at[peer_of(step)],
            dst_ref=arrived_tails.at[me],
            send_sem=tail_send_sems.at[step],
            recv_sem=tail_recv_sems.at[step],
            device_id=(peer_of(step), place),
            device_id_type=MESH,
        )

    def row_copy(step):
        return pltpu.make_async_remote_copy(
            src_ref=staged_rows.at[peer_of(step)],
            dst_ref=arrived_rows.at[me],
            send_sem=row_send_sems.at[step],
            recv_sem=row_recv_sems.at[step],
            device_id=(peer_of(step), place),
            device_id_type=MESH,
        )

    def pair_copy(chunk):
        return pltpu.make_async_remote_copy(
            src_ref=pair_send.at[chunk],
            dst_ref=pair_recv.at[chunk],
            send_sem=pair_send_sems.at[chunk],
            recv_sem=pair_recv_sems.at[chunk],
            device_id=(me, other),
            device_id_type=MESH,
        )

    def chip_copy(chunk, step):
        return pltpu.make_async_remote_copy(
            src_ref=chip_send.at[chunk, step - 1],
            dst_ref=chip_recv.at[chunk, step - 1],
            send_sem=chip_send_sems.at[chunk, step - 1],
            recv_sem=chip_recv_sems.at[chunk, step - 1],
            device_id=(me, chip_of(step) * CORES + core),
            device_id_type=MESH,
        )

    def send_tails(step, carry):
        tail_copy(step).start()
        return carry

    lax.fori_loop(1, groups, send_tails, 0)

    def widen(branch, carry):
        for i in range(new_count):
            both = fresh_ref[branch, i].astype(jnp.float32)
            for kind in range(2):
                fresh_wide[kind, i, pl.ds(branch, 1)] = both[kind : kind + 1]
        return carry

    lax.fori_loop(0, branches_here, widen, 0)
    load_cache.wait()
    load_proj.wait()

    def project(chunk):
        first = pl.multiple_of(chunk * spans, spans)
        lhs = jnp.concatenate([heads[i, pl.ds(first, spans)] for i in range(new_count)], axis=0)
        for y in range(chips):
            column = pl.multiple_of((y * CORES + core) * width, width)
            own[chunk, y] = jnp.dot(
                lhs, proj[:, pl.ds(column, width)], preferred_element_type=jnp.float32
            )
            column = pl.multiple_of((y * CORES + CORES - 1 - core) * width, width)
            pair_send[chunk, y] = jnp.dot(
                lhs, proj[:, pl.ds(column, width)], preferred_element_type=jnp.float32
            ).astype(pair_send.dtype)
        pair_copy(chunk).start()

    def exchange(chunk):
        pair_copy(chunk).wait()
        for step in range(1, chips):
            y = chip_of(step)
            both = own[chunk, y] + pair_recv[chunk, y].astype(jnp.float32)
            chip_send[chunk, step - 1] = both.astype(chip_send.dtype)
            chip_copy(chunk, step).start()

    def finish(chunk):
        first = pl.multiple_of(chunk * spans, spans)
        summed = own[chunk, chip] + pair_recv[chunk, chip].astype(jnp.float32)
        for step in range(1, chips):
            chip_copy(chunk, step).wait()
            summed += chip_recv[chunk, step - 1].astype(jnp.float32)
        for i in range(new_count):
            rows = summed[i * spans : (i + 1) * spans]
            rows += residual_ref[i, pl.ds(first, spans)].astype(jnp.float32)
            rows_out[i, pl.ds(first, spans)] = rows.astype(rows_out.dtype)
            for at in range(0, width, HEAD):
                wide_rows[pl.ds(first, spans), i * (width // HEAD) + at // HEAD] = rows[
                    :, at : at + HEAD
                ]

    def work(chunk, carry):
        def tile(index, inner):
            first = pl.multiple_of((chunk * TILES + index) * GROUP, GROUP)
            attend_tile(
                first, query_ref, cache, tails, fresh_wide, length_ref, second_ref, heads, scores
            )
            return inner

        lax.fori_loop(0, TILES, tile, 0)

        @pl.when(chunk > 0)
        def _():
            exchange(chunk - 1)

        project(chunk)
        return carry

    lax.fori_loop(0, chunks, work, 0)
    exchange(chunks - 1)

    def settle(branch, carry):
        keep = stay_ref[branch] > 0
        length = branch_length_ref[branch]
        for kind in range(2):
            rows = written_rows(tails[branch, kind], fresh_of(fresh_ref, branch, kind), length)
            tails[branch, kind] = jnp.where(keep, rows, jnp.zeros_like(rows))
        return carry

    def finish_chunk(chunk, carry):
        finish(chunk)
        return carry

    wide_rows[...] = jnp.zeros_like(wide_rows)
    lax.fori_loop(0, chunks, finish_chunk, 0)

    def pack_rows(slot, carry):
        staged_rows[slot // 2, slot % 2] = wide_rows[take_ref[slot]].astype(staged_rows.dtype)
        return carry

    lax.fori_loop(0, groups * 2, pack_rows, 0)

    def send_rows(step, carry):
        row_copy(step).start()
        return carry

    lax.fori_loop(1, groups, send_rows, 0)
    lax.fori_loop(0, branches_here, settle, 0)
    store_home = pltpu.make_async_copy(tails, home_out, load_sems.at[3])
    store_home.start()
    store_home.wait()

    def drain(step, carry):
        row_copy(step).wait()
        tail_copy(step).wait()
        return carry

    lax.fori_loop(1, groups, drain, 0)


def block(take, stay, lengths, queries, residual, fresh, length_rows, second, tails, cache, proj):
    groups, chips = lax.axis_size("dp"), lax.axis_size("tensor") // CORES
    new_count, branches_here, width = queries.shape
    spans = GROUP * TILES
    chunks = branches_here // spans
    rows = new_count * (width // HEAD) * GROUP
    kind = queries.dtype
    smem = pl.BlockSpec(memory_space=pltpu.SMEM)
    vmem = pl.BlockSpec(memory_space=pltpu.VMEM)
    hbm = pl.BlockSpec(memory_space=pl.ANY)
    flops = 8 * new_count * branches_here * (width // HEAD) * cache.shape[2] * HEAD
    dma = pltpu.SemaphoreType.DMA

    def body(*refs):
        block_kernel(groups, chips, *refs)

    return pl.pallas_call(
        body,
        out_shape=[
            jax.ShapeDtypeStruct(queries.shape, kind),
            jax.ShapeDtypeStruct((groups, 2, ROW, HEAD), kind),
            jax.ShapeDtypeStruct((groups, 2) + tails.shape[1:], kind),
            jax.ShapeDtypeStruct(tails.shape, kind),
        ],
        in_specs=[smem] * 3 + [vmem] * 5 + [hbm] * 3,
        out_specs=[vmem, hbm, hbm, hbm],
        scratch_shapes=[
            pltpu.VMEM(tails.shape, kind),
            pltpu.VMEM(cache.shape, kind),
            pltpu.VMEM(proj.shape, kind),
            pltpu.VMEM((groups, 2) + tails.shape[1:], kind),
            pltpu.VMEM((groups, 2, ROW, HEAD), kind),
            pltpu.VMEM((2, new_count, branches_here, HEAD), jnp.float32),
            pltpu.VMEM((rows, cache.shape[2]), jnp.float32),
            pltpu.VMEM(queries.shape, kind),
            pltpu.VMEM((chunks, chips, new_count * spans, width), jnp.float32),
            pltpu.VMEM((chunks, chips, new_count * spans, width), kind),
            pltpu.VMEM((chunks, chips, new_count * spans, width), kind),
            pltpu.VMEM((chunks, chips - 1, new_count * spans, width), kind),
            pltpu.VMEM((chunks, chips - 1, new_count * spans, width), kind),
            pltpu.VMEM((branches_here, ROW, HEAD), jnp.float32),
            dma((4,)),
            dma((groups,)),
            dma((groups,)),
            dma((groups,)),
            dma((groups,)),
            dma((chunks,)),
            dma((chunks,)),
            dma((chunks, chips - 1)),
            dma((chunks, chips - 1)),
        ],
        cost_estimate=pl.CostEstimate(
            flops=flops, bytes_accessed=20 * MIB, transcendentals=flops // 1024
        ),
        compiler_params=pltpu.CompilerParams(
            collective_id=0, has_side_effects=True, vmem_limit_bytes=52 * MIB
        ),
    )(take, lengths, stay, queries, residual, fresh, length_rows, second, tails, cache, proj)


def place_kernel(
    take_ref,
    keep_ref,
    rows_ref,
    arrived_rows_ref,
    home_ref,
    arrived_ref,
    mixed_ref,
    out_ref,
    blank,
    stage,
    sems,
    home_sem,
):
    incoming = take_ref.shape[0]
    new_count, first, width = rows_ref.shape
    lines = new_count * (width // HEAD)
    copy_home = pltpu.make_async_copy(home_ref, out_ref.at[pl.ds(0, first)], home_sem)
    copy_home.start()
    blank[...] = jnp.zeros_like(blank)

    def start(row, carry):
        source = take_ref[row]

        @pl.when(source >= 0)
        def _():
            pltpu.make_async_copy(
                arrived_ref.at[source], out_ref.at[first + row], sems.at[row]
            ).start()

        @pl.when(source < 0)
        def _():
            pltpu.make_async_copy(blank, out_ref.at[first + row], sems.at[row]).start()

        return carry

    def stage_row(row, carry):
        source = take_ref[row]
        value = arrived_rows_ref[jnp.maximum(source, 0)].astype(jnp.float32)
        value = jnp.where(source >= 0, value, 0.0)
        for line in range(lines):
            stage[line, pl.ds(row, 1)] = value[line : line + 1]
        return carry

    def done(row, carry):
        pltpu.make_async_copy(blank, out_ref.at[first + row], sems.at[row]).wait()
        return carry

    lax.fori_loop(0, incoming, start, 0)
    lax.fori_loop(0, incoming, stage_row, 0)
    keep = jnp.concatenate([keep_ref[...]] * (width // HEAD), axis=1) > 0
    for i in range(new_count):
        rows = rows_ref[i]
        mixed_ref[i, :first] = jnp.where(keep, rows, jnp.zeros_like(rows))
        for at in range(0, width, HEAD):
            line = i * (width // HEAD) + at // HEAD
            mixed_ref[i, first:, at : at + HEAD] = stage[line, :incoming].astype(mixed_ref.dtype)
    lax.fori_loop(0, incoming, done, 0)
    copy_home.wait()


def place(take, keep, rows, arrived_rows, home, arrived):
    incoming = take.shape[0]
    new_count, branches_here, width = rows.shape
    slots = branches_here + incoming
    smem = pl.BlockSpec(memory_space=pltpu.SMEM)
    vmem = pl.BlockSpec(memory_space=pltpu.VMEM)
    hbm = pl.BlockSpec(memory_space=pl.ANY)
    return pl.pallas_call(
        place_kernel,
        out_shape=[
            jax.ShapeDtypeStruct((new_count, slots, width), rows.dtype),
            jax.ShapeDtypeStruct((slots,) + home.shape[1:], home.dtype),
        ],
        in_specs=[smem, vmem, vmem, vmem, hbm, hbm],
        out_specs=[vmem, hbm],
        scratch_shapes=[
            pltpu.VMEM(home.shape[1:], home.dtype),
            pltpu.VMEM((new_count * (width // HEAD), incoming + 1, HEAD), jnp.float32),
            pltpu.SemaphoreType.DMA((incoming,)),
            pltpu.SemaphoreType.DMA(()),
        ],
        compiler_params=pltpu.CompilerParams(vmem_limit_bytes=8 * MIB),
    )(take, keep, rows, arrived_rows, home, arrived)


def routing(moves, self_index, branches_here, groups, incoming):
    branch_ids, source, target = moves[:, 0], moves[:, 1], moves[:, 2]
    entries = jnp.arange(moves.shape[0], dtype=jnp.int32)
    earlier = entries[None, :] < entries[:, None]
    same_target = earlier & (target[None, :] == target[:, None])
    arrival = jnp.sum(same_target.astype(jnp.int32), axis=1)
    rank = jnp.sum((same_target & (source[None, :] == source[:, None])).astype(jnp.int32), axis=1)
    local_slot = branch_ids - self_index * branches_here
    slots = jnp.arange(groups * 2, dtype=jnp.int32)
    sent = (source == self_index)[None, :] & ((target * 2 + rank)[None, :] == slots[:, None])
    take = jnp.sum(jnp.where(sent, local_slot[None, :], 0), axis=1)
    rows = jnp.arange(incoming, dtype=jnp.int32)
    placed = (target == self_index)[None, :] & (arrival[None, :] == rows[:, None])
    put = jnp.sum(jnp.where(placed, (source * 2 + rank + 1)[None, :], 0), axis=1) - 1
    here = jnp.arange(branches_here, dtype=jnp.int32)
    leaving = jnp.sum((local_slot[None, :] == here[:, None]).astype(jnp.int32), axis=1)
    stay = (leaving == 0).astype(jnp.int32)
    return take, put, stay


def on_device(queries, prompt_cache, tails, fresh, residual, out_proj, lengths, prompt_of, moves):
    groups = lax.axis_size("dp")
    self_index = lax.axis_index("dp")
    branches_here = queries.shape[0]
    take, put, stay = routing(moves, self_index, branches_here, groups, groups - 1)

    def across(values):
        return jnp.broadcast_to(values[:, None], (branches_here, HEAD))

    rows, arrived_rows, arrived_tails, home = block(
        take,
        stay,
        lengths,
        jnp.transpose(queries, (1, 0, 2)),
        jnp.transpose(residual, (1, 0, 2)),
        fresh,
        across(lengths),
        across(prompt_of - self_index * prompt_cache.shape[0]),
        tails,
        prompt_cache,
        out_proj,
    )
    mixed, tails_out = place(
        put,
        across(stay),
        rows,
        arrived_rows.reshape((groups * 2,) + arrived_rows.shape[2:]),
        home,
        arrived_tails.reshape((groups * 2,) + arrived_tails.shape[2:]),
    )
    return (jnp.transpose(mixed, (1, 0, 2)), tails_out)


def solution(mesh):
    in_specs = (
        P("dp", None, "tensor"),
        P("dp", None, None, "tensor"),
        P("dp", None, None, "tensor"),
        P("dp", None, None, "tensor"),
        P("dp", None, "tensor"),
        P("tensor", None),
        P("dp"),
        P("dp"),
        P(),
    )
    out_specs = (P("dp", None, "tensor"), P("dp", None, None, "tensor"))
    return jax.shard_map(
        on_device, mesh=mesh, in_specs=in_specs, out_specs=out_specs, check_vma=False
    )
```

```python
import math

import jax
import jax.numpy as jnp
from jax import lax
from jax.experimental import pallas as pl
from jax.experimental.pallas import tpu as pltpu
from jax.sharding import PartitionSpec as P

HEAD = 128
GROUP = 16
TILES = 2
CHUNK = 512
CORES = 2
ROW = 16
MIB = 1 << 20
HOME_PARTS = 6
MESH = pl.DeviceIdType.MESH


def written_rows(rows, fresh, length):
    at = lax.broadcasted_iota(jnp.int32, rows.shape, 0)
    wide = rows.astype(jnp.float32)
    for i, line in enumerate(fresh):
        wide = jnp.where(at == length + i, line, wide)
    return wide.astype(rows.dtype)


def fresh_of(fresh_ref, branch, kind):
    pairs = [fresh_ref[branch, i].astype(jnp.float32) for i in range(fresh_ref.shape[1])]
    return [pair[kind : kind + 1] for pair in pairs]


def attend_tile(first, query_ref, cache, tails, fresh_wide, length_ref, second_ref, heads, scores):
    new_count = query_ref.shape[0]
    share = query_ref.shape[2] // HEAD
    keys = cache.shape[2]
    tail_rows = tails.shape[2]
    tail_keys = GROUP * tail_rows
    blocks = new_count * share
    rows = blocks * GROUP
    factor = math.log2(math.e) / math.sqrt(HEAD)
    contract_last = (((1,), (1,)), ((), ()))

    def lanes(op, value, carry):
        for at in range(0, value.shape[1], HEAD):
            carry = op(carry, value[:, at : at + HEAD])
        return carry

    def fresh_block(kind):
        parts = [fresh_wide[kind, i, pl.ds(first, GROUP)] for i in range(new_count)]
        parts.append(jnp.zeros((HEAD - new_count * GROUP, HEAD), jnp.float32))
        return jnp.concatenate(parts, axis=0).astype(jnp.bfloat16)

    query = jnp.concatenate(
        [
            query_ref[i, pl.ds(first, GROUP), h * HEAD : (h + 1) * HEAD]
            for i in range(new_count)
            for h in range(share)
        ],
        axis=0,
    )
    second = jnp.concatenate([second_ref[pl.ds(first, GROUP)]] * blocks, axis=0) > 0
    nothing = jnp.zeros_like(query)
    both = jnp.concatenate(
        [jnp.where(second, nothing, query), jnp.where(second, query, nothing)], axis=1
    )
    top = jnp.full((rows, HEAD), -jnp.inf, jnp.float32)
    for at in range(0, keys, CHUNK):
        key_block = jnp.concatenate(
            [cache[0, 0, at : at + CHUNK], cache[1, 0, at : at + CHUNK]], axis=1
        )
        block = lax.dot_general(both, key_block, contract_last, preferred_element_type=jnp.float32)
        scores[:, at : at + CHUNK] = block
        top = lanes(jnp.maximum, block, top)
    tail_scores = lax.dot_general(
        query,
        tails[pl.ds(first, GROUP), 0].reshape(tail_keys, HEAD),
        contract_last,
        preferred_element_type=jnp.float32,
    )
    length = jnp.concatenate([length_ref[pl.ds(first, GROUP)]] * blocks, axis=0)
    row_at = lax.broadcasted_iota(jnp.int32, (rows, HEAD), 0)
    key_at = lax.broadcasted_iota(jnp.int32, (rows, HEAD), 1)
    held = []
    for at in range(0, tail_keys, HEAD):
        seen = (row_at % GROUP == (key_at + at) // tail_rows) & (key_at % tail_rows < length)
        held.append(jnp.where(seen, tail_scores[:, at : at + HEAD], -jnp.inf))
    tail_scores = jnp.concatenate(held, axis=1)
    fresh_scores = lax.dot_general(
        query, fresh_block(0), contract_last, preferred_element_type=jnp.float32
    )
    seen = (row_at % GROUP == key_at % GROUP) & (key_at // GROUP <= row_at // (GROUP * share))
    fresh_scores = jnp.where(seen, fresh_scores, -jnp.inf)
    top = jnp.maximum(lanes(jnp.maximum, tail_scores, top), fresh_scores)
    top = jnp.max(top, axis=1, keepdims=True)
    total = jnp.zeros((rows, HEAD), jnp.float32)
    pair = jnp.zeros((rows, 2 * HEAD), jnp.float32)
    for at in range(0, keys, CHUNK):
        expo = jnp.exp2((scores[:, at : at + CHUNK] - top) * factor)
        total = lanes(jnp.add, expo, total)
        value_block = jnp.concatenate(
            [cache[0, 1, at : at + CHUNK], cache[1, 1, at : at + CHUNK]], axis=1
        )
        pair += jnp.dot(expo.astype(jnp.bfloat16), value_block, preferred_element_type=jnp.float32)
    mixed = jnp.where(second, pair[:, HEAD:], pair[:, :HEAD])
    expo = jnp.exp2((tail_scores - top) * factor)
    total = lanes(jnp.add, expo, total)
    mixed += jnp.dot(
        expo.astype(jnp.bfloat16),
        tails[pl.ds(first, GROUP), 1].reshape(tail_keys, HEAD),
        preferred_element_type=jnp.float32,
    )
    expo = jnp.exp2((fresh_scores - top) * factor)
    total += expo
    mixed += jnp.dot(
        expo.astype(jnp.bfloat16), fresh_block(1), preferred_element_type=jnp.float32
    )
    result = (mixed / jnp.sum(total, axis=1, keepdims=True)).astype(heads.dtype)
    for i in range(new_count):
        for h in range(share):
            at = (i * share + h) * GROUP
            heads[i, pl.ds(first, GROUP), h * HEAD : (h + 1) * HEAD] = result[at : at + GROUP]


def find_slots(me, groups, branches_here, moves, slot_table, keep_rows):
    branch, source, target = (moves[at : at + 1] for at in range(3))
    entries = moves.shape[1]
    group = lax.broadcasted_iota(jnp.int32, (groups, entries), 0)
    entry = lax.broadcasted_iota(jnp.int32, (groups, entries), 1)
    local = branch - me * branches_here
    far = entries * HEAD
    code = jnp.where((source == me) & (target == group), entry * HEAD + local, -1)
    last = jnp.max(code, axis=1, keepdims=True)
    first = jnp.min(jnp.where(code >= 0, code, far), axis=1, keepdims=True)
    sent = [jnp.where(first < far, first % HEAD, 0), jnp.where(last >= 0, last % HEAD, 0)]
    here = target == me
    code = jnp.where(here & (source == group), entry, -1)
    last = jnp.max(code, axis=1, keepdims=True)
    first = jnp.min(jnp.where(code >= 0, code, entries), axis=1, keepdims=True)

    def arrival(at):
        return jnp.sum(jnp.where(here & (entry < at), 1, 0), axis=1, keepdims=True)

    arrive = [
        jnp.where(last >= 0, arrival(first), -1),
        jnp.where(last > first, arrival(last), -1),
    ]
    column = lax.broadcasted_iota(jnp.int32, slot_table.shape, 1)
    table = jnp.broadcast_to(arrival(entries), slot_table.shape)
    for at, value in enumerate(sent + arrive):
        table = jnp.where(column == at, value, table)
    slot_table[...] = table
    row = lax.broadcasted_iota(jnp.int32, (branches_here, entries), 0)
    gone = jnp.where((source == me) & (local == row), 1, 0)
    gone = jnp.max(gone, axis=1, keepdims=True)
    keep_rows[...] = jnp.broadcast_to(1 - gone, keep_rows.shape)


def spread(scalars, rows, base=0):
    def step(at, carry):
        rows[pl.ds(at, 1)] = jnp.full((1, rows.shape[1]), scalars[at] - base, jnp.int32)
        return carry

    lax.fori_loop(0, rows.shape[0], step, 0)


def block_kernel(
    groups,
    chips,
    lengths_in,
    prompt_of_in,
    moves_in,
    query_in,
    residual_in,
    fresh_in,
    tails_in,
    cache_in,
    proj_in,
    rows_out,
    arrived_rows,
    arrived_tails,
    home_out,
    slots_out,
    branch_length_ref,
    branch_prompt_ref,
    moves,
    slot_table,
    slot_scalars,
    keep_rows,
    length_ref,
    second_ref,
    query_ref,
    residual_ref,
    fresh_ref,
    tails,
    cache,
    proj,
    staged,
    staged_rows,
    fresh_wide,
    scores,
    heads,
    own,
    pair_send,
    pair_recv,
    chip_send,
    chip_recv,
    wide_rows,
    load_sems,
    tail_send_sems,
    tail_recv_sems,
    row_send_sems,
    row_recv_sems,
    pair_send_sems,
    pair_recv_sems,
    chip_send_sems,
    chip_recv_sems,
):
    new_count, branches_here, width = query_ref.shape
    me = lax.axis_index("dp")
    place = lax.axis_index("tensor")
    chip, core = place // CORES, place % CORES
    other = chip * CORES + (CORES - 1 - core)
    spans = GROUP * TILES
    chunks = branches_here // spans

    def peer_of(step):
        return lax.rem(me + step, groups)

    def chip_of(step):
        return lax.rem(chip + step, chips)

    barrier = pltpu.get_barrier_semaphore()

    def greet(step, carry):
        pl.semaphore_signal(
            barrier, inc=1, device_id=(peer_of(step), place), device_id_type=MESH
        )
        return carry

    load_lengths = pltpu.make_async_copy(lengths_in, branch_length_ref, load_sems.at[8])
    load_prompts = pltpu.make_async_copy(prompt_of_in, branch_prompt_ref, load_sems.at[9])
    load_moves = pltpu.make_async_copy(moves_in, moves, load_sems.at[0])
    load_tails = pltpu.make_async_copy(tails_in, tails, load_sems.at[1])
    load_fresh = pltpu.make_async_copy(fresh_in, fresh_ref, load_sems.at[2])
    load_query = pltpu.make_async_copy(query_in, query_ref, load_sems.at[3])
    load_residual = pltpu.make_async_copy(residual_in, residual_ref, load_sems.at[4])
    load_cache = pltpu.make_async_copy(cache_in, cache, load_sems.at[5])
    load_proj = pltpu.make_async_copy(proj_in, proj, load_sems.at[6])
    load_moves.start()
    load_tails.start()
    load_fresh.start()
    load_lengths.start()
    load_prompts.start()
    lax.fori_loop(1, groups, greet, 0)
    pl.semaphore_signal(barrier, inc=1, device_id=(me, other), device_id_type=MESH)
    for step in range(1, chips):
        pl.semaphore_signal(
            barrier,
            inc=1,
            device_id=(me, chip_of(step) * CORES + core),
            device_id_type=MESH,
        )

    load_query.start()
    load_residual.start()
    load_cache.start()
    load_proj.start()
    load_moves.wait()
    find_slots(me, groups, branches_here, moves, slot_table, keep_rows)
    load_slots = pltpu.make_async_copy(slot_table, slot_scalars, load_sems.at[7])
    load_slots.start()
    load_slots.wait()
    load_tails.wait()
    load_fresh.wait()
    load_lengths.wait()
    load_prompts.wait()

    def pack(slot, carry):
        branch = slot_scalars[slot // 2, slot % 2]
        length = branch_length_ref[branch]
        for kind in range(2):
            staged[slot // 2, slot % 2, kind] = written_rows(
                tails[branch, kind], fresh_of(fresh_ref, branch, kind), length
            )
        return carry

    lax.fori_loop(0, groups * 2, pack, 0)
    pl.semaphore_wait(barrier, groups - 1 + 1 + chips - 1)

    def tail_copy(step):
        return pltpu.make_async_remote_copy(
            src_ref=staged.at[peer_of(step)],
            dst_ref=arrived_tails.at[me],
            send_sem=tail_send_sems.at[step],
            recv_sem=tail_recv_sems.at[step],
            device_id=(peer_of(step), place),
            device_id_type=MESH,
        )

    def row_copy(step):
        return pltpu.make_async_remote_copy(
            src_ref=staged_rows.at[peer_of(step)],
            dst_ref=arrived_rows.at[me],
            send_sem=row_send_sems.at[step],
            recv_sem=row_recv_sems.at[step],
            device_id=(peer_of(step), place),
            device_id_type=MESH,
        )

    def pair_copy(chunk):
        return pltpu.make_async_remote_copy(
            src_ref=pair_send.at[chunk],
            dst_ref=pair_recv.at[chunk],
            send_sem=pair_send_sems.at[chunk],
            recv_sem=pair_recv_sems.at[chunk],
            device_id=(me, other),
            device_id_type=MESH,
        )

    def chip_copy(chunk, step):
        return pltpu.make_async_remote_copy(
            src_ref=chip_send.at[chunk, step - 1],
            dst_ref=chip_recv.at[chunk, step - 1],
            send_sem=chip_send_sems.at[chunk, step - 1],
            recv_sem=chip_recv_sems.at[chunk, step - 1],
            device_id=(me, chip_of(step) * CORES + core),
            device_id_type=MESH,
        )

    def send_tails(step, carry):
        tail_copy(step).start()
        return carry

    lax.fori_loop(1, groups, send_tails, 0)

    def widen(branch, carry):
        for i in range(new_count):
            both = fresh_ref[branch, i].astype(jnp.float32)
            for kind in range(2):
                fresh_wide[kind, i, pl.ds(branch, 1)] = both[kind : kind + 1]
        return carry

    lax.fori_loop(0, branches_here, widen, 0)
    spread(branch_length_ref, length_ref)
    spread(branch_prompt_ref, second_ref, me * cache.shape[0])
    store_slots = pltpu.make_async_copy(slot_table, slots_out, load_sems.at[0])
    store_slots.start()
    store_slots.wait()
    load_query.wait()
    load_residual.wait()
    load_cache.wait()
    load_proj.wait()

    def project(chunk):
        first = pl.multiple_of(chunk * spans, spans)
        lhs = jnp.concatenate([heads[i, pl.ds(first, spans)] for i in range(new_count)], axis=0)
        for y in range(chips):
            column = pl.multiple_of((y * CORES + core) * width, width)
            own[chunk, y] = jnp.dot(
                lhs, proj[:, pl.ds(column, width)], preferred_element_type=jnp.float32
            )
            column = pl.multiple_of((y * CORES + CORES - 1 - core) * width, width)
            pair_send[chunk, y] = jnp.dot(
                lhs, proj[:, pl.ds(column, width)], preferred_element_type=jnp.float32
            ).astype(pair_send.dtype)
        pair_copy(chunk).start()

    def exchange(chunk):
        pair_copy(chunk).wait()
        for step in range(1, chips):
            y = chip_of(step)
            both = own[chunk, y] + pair_recv[chunk, y].astype(jnp.float32)
            chip_send[chunk, step - 1] = both.astype(chip_send.dtype)
            chip_copy(chunk, step).start()

    def finish(chunk):
        first = pl.multiple_of(chunk * spans, spans)
        summed = own[chunk, chip] + pair_recv[chunk, chip].astype(jnp.float32)
        for step in range(1, chips):
            chip_copy(chunk, step).wait()
            summed += chip_recv[chunk, step - 1].astype(jnp.float32)
        for i in range(new_count):
            rows = summed[i * spans : (i + 1) * spans]
            rows += residual_ref[i, pl.ds(first, spans)].astype(jnp.float32)
            keep = jnp.concatenate([keep_rows[pl.ds(first, spans)]] * (width // HEAD), axis=1) > 0
            rows_out[i, pl.ds(first, spans)] = jnp.where(keep, rows, 0.0).astype(rows_out.dtype)
            for at in range(0, width, HEAD):
                wide_rows[pl.ds(first, spans), i * (width // HEAD) + at // HEAD] = rows[
                    :, at : at + HEAD
                ]

    def work(chunk, carry):
        def tile(index, inner):
            first = pl.multiple_of((chunk * TILES + index) * GROUP, GROUP)
            attend_tile(
                first, query_ref, cache, tails, fresh_wide, length_ref, second_ref, heads, scores
            )
            return inner

        lax.fori_loop(0, TILES, tile, 0)

        @pl.when(chunk > 0)
        def _():
            exchange(chunk - 1)

        project(chunk)
        return carry

    lax.fori_loop(0, chunks, work, 0)
    exchange(chunks - 1)

    def settle(branch, carry):
        keep = jnp.broadcast_to(keep_rows[pl.ds(branch, 1)], tails.shape[2:]) > 0
        length = branch_length_ref[branch]
        for kind in range(2):
            rows = written_rows(tails[branch, kind], fresh_of(fresh_ref, branch, kind), length)
            rows = jnp.where(keep, rows.astype(jnp.float32), 0.0)
            tails[branch, kind] = rows.astype(tails.dtype)
        return carry

    def finish_chunk(chunk, carry):
        finish(chunk)
        return carry

    wide_rows[...] = jnp.zeros_like(wide_rows)
    lax.fori_loop(0, chunks, finish_chunk, 0)

    def pack_rows(slot, carry):
        staged_rows[slot // 2, slot % 2] = wide_rows[
            slot_scalars[slot // 2, slot % 2]
        ].astype(staged_rows.dtype)
        return carry

    lax.fori_loop(0, groups * 2, pack_rows, 0)

    def send_rows(step, carry):
        row_copy(step).start()
        return carry

    lax.fori_loop(1, groups, send_rows, 0)
    lax.fori_loop(0, branches_here, settle, 0)
    store_home = pltpu.make_async_copy(tails, home_out, load_sems.at[1])
    store_home.start()
    store_home.wait()

    def drain(step, carry):
        row_copy(step).wait()
        tail_copy(step).wait()
        return carry

    lax.fori_loop(1, groups, drain, 0)


def block(*arrays):
    lengths, prompt_of, moves, queries, residual, fresh, tails, cache, proj = arrays
    groups, chips = lax.axis_size("dp"), lax.axis_size("tensor") // CORES
    new_count, branches_here, width = queries.shape
    spans = GROUP * TILES
    chunks = branches_here // spans
    rows = new_count * (width // HEAD) * GROUP
    kind = queries.dtype
    vmem = pl.BlockSpec(memory_space=pltpu.VMEM)
    hbm = pl.BlockSpec(memory_space=pl.ANY)
    flops = 8 * new_count * branches_here * (width // HEAD) * cache.shape[2] * HEAD
    dma = pltpu.SemaphoreType.DMA

    def body(*refs):
        block_kernel(groups, chips, *refs)

    return pl.pallas_call(
        body,
        out_shape=[
            pltpu.VMEM(queries.shape, kind),
            pltpu.VMEM((groups, 2, ROW, HEAD), kind),
            pltpu.VMEM((groups, 2) + tails.shape[1:], kind),
            pltpu.VMEM(tails.shape, kind),
            pltpu.VMEM((groups, HEAD), jnp.int32),
        ],
        in_specs=[pl.BlockSpec(memory_space=pltpu.HBM)] * 9,
        out_specs=[vmem, hbm, hbm, hbm, hbm],
        scratch_shapes=[
            pltpu.SMEM(lengths.shape, jnp.int32),
            pltpu.SMEM(prompt_of.shape, jnp.int32),
            pltpu.VMEM(moves.shape, jnp.int32),
            pltpu.VMEM((groups, HEAD), jnp.int32),
            pltpu.SMEM((groups, HEAD), jnp.int32),
            pltpu.VMEM((branches_here, HEAD), jnp.int32),
            pltpu.VMEM((branches_here, HEAD), jnp.int32),
            pltpu.VMEM((branches_here, HEAD), jnp.int32),
            pltpu.VMEM(queries.shape, kind),
            pltpu.VMEM(residual.shape, kind),
            pltpu.VMEM(fresh.shape, kind),
            pltpu.VMEM(tails.shape, kind),
            pltpu.VMEM(cache.shape, kind),
            pltpu.VMEM(proj.shape, kind),
            pltpu.VMEM((groups, 2) + tails.shape[1:], kind),
            pltpu.VMEM((groups, 2, ROW, HEAD), kind),
            pltpu.VMEM((2, new_count, branches_here, HEAD), jnp.float32),
            pltpu.VMEM((rows, cache.shape[2]), jnp.float32),
            pltpu.VMEM(queries.shape, kind),
            pltpu.VMEM((chunks, chips, new_count * spans, width), jnp.float32),
            pltpu.VMEM((chunks, chips, new_count * spans, width), kind),
            pltpu.VMEM((chunks, chips, new_count * spans, width), kind),
            pltpu.VMEM((chunks, chips - 1, new_count * spans, width), kind),
            pltpu.VMEM((chunks, chips - 1, new_count * spans, width), kind),
            pltpu.VMEM((branches_here, ROW, HEAD), jnp.float32),
            dma((10,)),
            dma((groups,)),
            dma((groups,)),
            dma((groups,)),
            dma((groups,)),
            dma((chunks,)),
            dma((chunks,)),
            dma((chunks, chips - 1)),
            dma((chunks, chips - 1)),
        ],
        cost_estimate=pl.CostEstimate(
            flops=flops, bytes_accessed=20 * MIB, transcendentals=flops // 1024
        ),
        compiler_params=pltpu.CompilerParams(
            collective_id=0, has_side_effects=True, vmem_limit_bytes=46 * MIB
        ),
    )(*(pltpu.with_memory_space_constraint(array, pltpu.HBM) for array in arrays))


def place_kernel(
    slots_ref,
    rows_in,
    arrived_rows_in,
    home_in,
    arrived_in,
    mixed_ref,
    out_ref,
    rows,
    arrived_rows,
    blank,
    stage,
    sems,
    load_sems,
):
    incoming = sems.shape[0]
    new_count, first, width = rows.shape
    lines = new_count * (width // HEAD)
    parts = load_sems.shape[0] - 2
    share = first // parts
    load_rows = pltpu.make_async_copy(rows_in, rows, load_sems.at[0])
    load_arrived = pltpu.make_async_copy(arrived_rows_in, arrived_rows, load_sems.at[1])

    def home_copy(part):
        at = pl.ds(part * share, share)
        return pltpu.make_async_copy(home_in.at[at], out_ref.at[at], load_sems.at[2 + part])

    def row_copy(source, row):
        return pltpu.make_async_copy(source, out_ref.at[first + row], sems.at[row])

    load_arrived.start()
    load_rows.start()
    for part in range(parts):
        home_copy(part).start()
    blank[...] = jnp.zeros_like(blank)
    stage[...] = jnp.zeros_like(stage)
    count = slots_ref[0, 4]

    def start(slot, carry):
        row = slots_ref[slot // 2, 2 + slot % 2]

        @pl.when(row >= 0)
        def _():
            row_copy(arrived_in.at[slot], row).start()

        return carry

    def clear(row, carry):
        row_copy(blank, row).start()
        return carry

    def stage_row(slot, carry):
        row = slots_ref[slot // 2, 2 + slot % 2]

        @pl.when(row >= 0)
        def _():
            value = arrived_rows[slot].astype(jnp.float32)
            for line in range(lines):
                stage[line, pl.ds(row, 1)] = value[line : line + 1]

        return carry

    def done(row, carry):
        row_copy(blank, row).wait()
        return carry

    lax.fori_loop(0, arrived_in.shape[0], start, 0)
    lax.fori_loop(count, incoming, clear, 0)
    load_arrived.wait()
    lax.fori_loop(0, arrived_in.shape[0], stage_row, 0)
    load_rows.wait()
    for i in range(new_count):
        mixed_ref[i, :first] = rows[i]
        for at in range(0, width, HEAD):
            line = i * (width // HEAD) + at // HEAD
            mixed_ref[i, first:, at : at + HEAD] = stage[line, :incoming].astype(mixed_ref.dtype)
    lax.fori_loop(0, incoming, done, 0)
    for part in range(parts):
        home_copy(part).wait()


def place(slot_table, rows, arrived_rows, home, arrived, incoming):
    new_count, branches_here, width = rows.shape
    slots = branches_here + incoming
    smem = pl.BlockSpec(memory_space=pltpu.SMEM)
    vmem = pl.BlockSpec(memory_space=pltpu.VMEM)
    hbm = pl.BlockSpec(memory_space=pl.ANY)
    return pl.pallas_call(
        place_kernel,
        out_shape=[
            jax.ShapeDtypeStruct((new_count, slots, width), rows.dtype),
            jax.ShapeDtypeStruct((slots,) + home.shape[1:], home.dtype),
        ],
        in_specs=[smem] + [hbm] * 4,
        out_specs=[vmem, hbm],
        scratch_shapes=[
            pltpu.VMEM(rows.shape, rows.dtype),
            pltpu.VMEM(arrived_rows.shape, rows.dtype),
            pltpu.VMEM(home.shape[1:], home.dtype),
            pltpu.VMEM((new_count * (width // HEAD), incoming + 1, HEAD), jnp.float32),
            pltpu.SemaphoreType.DMA((incoming,)),
            pltpu.SemaphoreType.DMA((2 + HOME_PARTS,)),
        ],
        compiler_params=pltpu.CompilerParams(vmem_limit_bytes=8 * MIB),
    )(slot_table, rows, arrived_rows, home, arrived)


def on_device(queries, prompt_cache, tails, fresh, residual, out_proj, lengths, prompt_of, moves):
    groups = lax.axis_size("dp")
    rows, arrived_rows, arrived_tails, home, slot_table = block(
        lengths,
        prompt_of,
        jnp.transpose(moves),
        jnp.transpose(queries, (1, 0, 2)),
        jnp.transpose(residual, (1, 0, 2)),
        fresh,
        tails,
        prompt_cache,
        out_proj,
    )
    mixed, tails_out = place(
        slot_table,
        rows,
        arrived_rows.reshape((groups * 2,) + arrived_rows.shape[2:]),
        home,
        arrived_tails.reshape((groups * 2,) + arrived_tails.shape[2:]),
        groups - 1,
    )
    return (jnp.transpose(mixed, (1, 0, 2)), tails_out)


def solution(mesh):
    in_specs = (
        P("dp", None, "tensor"),
        P("dp", None, None, "tensor"),
        P("dp", None, None, "tensor"),
        P("dp", None, None, "tensor"),
        P("dp", None, "tensor"),
        P("tensor", None),
        P("dp"),
        P("dp"),
        P(),
    )
    out_specs = (P("dp", None, "tensor"), P("dp", None, None, "tensor"))
    return jax.shard_map(
        on_device, mesh=mesh, in_specs=in_specs, out_specs=out_specs, check_vma=False
    )
```

```python
import math

import jax
import jax.numpy as jnp
from jax import lax
from jax.experimental import pallas as pl
from jax.experimental.pallas import tpu as pltpu
from jax.sharding import PartitionSpec as P

HEAD = 128
GROUP = 16
TILES = 2
CHUNK = 512
CORES = 2
ROW = 16
MIB = 1 << 20
PARTS = 4
MESH = pl.DeviceIdType.MESH


def wrapped(index, size):
    return jnp.where(index >= size, index - size, index)


def written_rows(rows, fresh, length):
    at = lax.broadcasted_iota(jnp.int32, rows.shape, 0)
    wide = rows.astype(jnp.float32)
    for i, line in enumerate(fresh):
        wide = jnp.where(at == length + i, line, wide)
    return wide.astype(rows.dtype)


def fresh_of(fresh_ref, branch, kind):
    pairs = [fresh_ref[branch, i].astype(jnp.float32) for i in range(fresh_ref.shape[1])]
    return [pair[kind : kind + 1] for pair in pairs]


def attend_tile(first, query_ref, cache, tails, fresh_wide, length_ref, second_ref, heads, scores):
    new_count = query_ref.shape[0]
    share = query_ref.shape[2] // HEAD
    keys = cache.shape[2]
    tail_rows = tails.shape[2]
    tail_keys = GROUP * tail_rows
    blocks = new_count * share
    rows = blocks * GROUP
    factor = math.log2(math.e) / math.sqrt(HEAD)
    contract_last = (((1,), (1,)), ((), ()))

    def lanes(op, value, carry):
        for at in range(0, value.shape[1], HEAD):
            carry = op(carry, value[:, at : at + HEAD])
        return carry

    def fresh_block(kind):
        parts = [fresh_wide[kind, i, pl.ds(first, GROUP)] for i in range(new_count)]
        parts.append(jnp.zeros((HEAD - new_count * GROUP, HEAD), jnp.float32))
        return jnp.concatenate(parts, axis=0).astype(jnp.bfloat16)

    query = jnp.concatenate(
        [
            query_ref[i, pl.ds(first, GROUP), h * HEAD : (h + 1) * HEAD]
            for i in range(new_count)
            for h in range(share)
        ],
        axis=0,
    )
    second = jnp.concatenate([second_ref[pl.ds(first, GROUP)]] * blocks, axis=0) > 0
    nothing = jnp.zeros_like(query)
    both = jnp.concatenate(
        [jnp.where(second, nothing, query), jnp.where(second, query, nothing)], axis=1
    )
    top = jnp.full((rows, HEAD), -jnp.inf, jnp.float32)
    for at in range(0, keys, CHUNK):
        key_block = jnp.concatenate(
            [cache[0, 0, at : at + CHUNK], cache[1, 0, at : at + CHUNK]], axis=1
        )
        block = lax.dot_general(both, key_block, contract_last, preferred_element_type=jnp.float32)
        scores[:, at : at + CHUNK] = block
        top = lanes(jnp.maximum, block, top)
    tail_scores = lax.dot_general(
        query,
        tails[pl.ds(first, GROUP), 0].reshape(tail_keys, HEAD),
        contract_last,
        preferred_element_type=jnp.float32,
    )
    length = jnp.concatenate([length_ref[pl.ds(first, GROUP)]] * blocks, axis=0)
    row_at = lax.broadcasted_iota(jnp.int32, (rows, HEAD), 0)
    key_at = lax.broadcasted_iota(jnp.int32, (rows, HEAD), 1)
    held = []
    for at in range(0, tail_keys, HEAD):
        seen = (row_at % GROUP == (key_at + at) // tail_rows) & (key_at % tail_rows < length)
        held.append(jnp.where(seen, tail_scores[:, at : at + HEAD], -jnp.inf))
    tail_scores = jnp.concatenate(held, axis=1)
    fresh_scores = lax.dot_general(
        query, fresh_block(0), contract_last, preferred_element_type=jnp.float32
    )
    seen = (row_at % GROUP == key_at % GROUP) & (key_at // GROUP <= row_at // (GROUP * share))
    fresh_scores = jnp.where(seen, fresh_scores, -jnp.inf)
    top = jnp.maximum(lanes(jnp.maximum, tail_scores, top), fresh_scores)
    top = jnp.max(top, axis=1, keepdims=True)
    total = jnp.zeros((rows, HEAD), jnp.float32)
    pair = jnp.zeros((rows, 2 * HEAD), jnp.float32)
    for at in range(0, keys, CHUNK):
        expo = jnp.exp2((scores[:, at : at + CHUNK] - top) * factor)
        total = lanes(jnp.add, expo, total)
        value_block = jnp.concatenate(
            [cache[0, 1, at : at + CHUNK], cache[1, 1, at : at + CHUNK]], axis=1
        )
        pair += jnp.dot(expo.astype(jnp.bfloat16), value_block, preferred_element_type=jnp.float32)
    mixed = jnp.where(second, pair[:, HEAD:], pair[:, :HEAD])
    expo = jnp.exp2((tail_scores - top) * factor)
    total = lanes(jnp.add, expo, total)
    mixed += jnp.dot(
        expo.astype(jnp.bfloat16),
        tails[pl.ds(first, GROUP), 1].reshape(tail_keys, HEAD),
        preferred_element_type=jnp.float32,
    )
    expo = jnp.exp2((fresh_scores - top) * factor)
    total += expo
    mixed += jnp.dot(
        expo.astype(jnp.bfloat16), fresh_block(1), preferred_element_type=jnp.float32
    )
    result = (mixed / jnp.sum(total, axis=1, keepdims=True)).astype(heads.dtype)
    for i in range(new_count):
        for h in range(share):
            at = (i * share + h) * GROUP
            heads[i, pl.ds(first, GROUP), h * HEAD : (h + 1) * HEAD] = result[at : at + GROUP]


def find_slots(me, groups, branches_here, moves, slot_table, keep_rows):
    branch, source, target = (moves[at : at + 1] for at in range(3))
    entries = moves.shape[1]
    group = lax.broadcasted_iota(jnp.int32, (groups, entries), 0)
    entry = lax.broadcasted_iota(jnp.int32, (groups, entries), 1)
    local = branch - me * branches_here
    far = entries * HEAD
    code = jnp.where((source == me) & (target == group), entry * HEAD + local, -1)
    last = jnp.max(code, axis=1, keepdims=True)
    first = jnp.min(jnp.where(code >= 0, code, far), axis=1, keepdims=True)
    sent = [jnp.where(first < far, first % HEAD, 0), jnp.where(last >= 0, last % HEAD, 0)]
    here = target == me
    code = jnp.where(here & (source == group), entry, -1)
    last = jnp.max(code, axis=1, keepdims=True)
    first = jnp.min(jnp.where(code >= 0, code, entries), axis=1, keepdims=True)

    def arrival(at):
        return jnp.sum(jnp.where(here & (entry < at), 1, 0), axis=1, keepdims=True)

    square = (groups, groups)
    row = lax.broadcasted_iota(jnp.int32, square, 0)
    column = lax.broadcasted_iota(jnp.int32, square, 1)

    def flat(value):
        return jnp.sum(jnp.where(row == column, value, 0), axis=0, keepdims=True)

    once = flat(jnp.where(last >= 0, arrival(first), -1))
    twice = flat(jnp.where(last > first, arrival(last), -1))
    slot = jnp.where(once == row, column * 2, jnp.where(twice == row, column * 2 + 1, -1))
    sent.append(jnp.max(slot, axis=1, keepdims=True))
    column = lax.broadcasted_iota(jnp.int32, slot_table.shape, 1)
    table = jnp.zeros(slot_table.shape, jnp.int32)
    for at, value in enumerate(sent):
        table = jnp.where(column == at, value, table)
    slot_table[...] = table
    row = lax.broadcasted_iota(jnp.int32, (branches_here, entries), 0)
    gone = jnp.where((source == me) & (local == row), 1, 0)
    gone = jnp.max(gone, axis=1, keepdims=True)
    keep_rows[...] = jnp.broadcast_to(1 - gone, keep_rows.shape)


def spread(scalars, rows, base=0):
    def step(at, carry):
        rows[pl.ds(at, 1)] = jnp.full((1, rows.shape[1]), scalars[at] - base, jnp.int32)
        return carry

    lax.fori_loop(0, rows.shape[0], step, 0)


def block_kernel(
    groups,
    chips,
    lengths_in,
    prompt_of_in,
    moves_in,
    query_in,
    residual_in,
    fresh_in,
    tails_in,
    cache_in,
    proj_in,
    mixed_out,
    tails_out,
    arrived_rows,
    arrived_tails,
    stage,
    branch_length_ref,
    branch_prompt_ref,
    moves,
    slot_table,
    slot_scalars,
    keep_rows,
    length_ref,
    second_ref,
    query_ref,
    residual_ref,
    fresh_ref,
    tails,
    cache,
    proj,
    staged,
    staged_rows,
    fresh_wide,
    scores,
    heads,
    own,
    pair_send,
    pair_recv,
    chip_send,
    chip_recv,
    wide_rows,
    load_sems,
    tail_send_sems,
    tail_recv_sems,
    row_send_sems,
    row_recv_sems,
    pair_send_sems,
    pair_recv_sems,
    chip_send_sems,
    chip_recv_sems,
):
    new_count, branches_here, width = query_ref.shape
    me = lax.axis_index("dp")
    place = lax.axis_index("tensor")
    chip, core = place // CORES, place % CORES
    other = chip * CORES + (CORES - 1 - core)
    spans = GROUP * TILES
    chunks = branches_here // spans

    def peer_of(step):
        return wrapped(me + step, groups)

    def chip_of(step):
        return wrapped(chip + step, chips)

    barrier = pltpu.get_barrier_semaphore()

    def greet(step, carry):
        pl.semaphore_signal(
            barrier, inc=1, device_id=(peer_of(step), place), device_id_type=MESH
        )
        return carry

    load_lengths = pltpu.make_async_copy(lengths_in, branch_length_ref, load_sems.at[8])
    load_prompts = pltpu.make_async_copy(prompt_of_in, branch_prompt_ref, load_sems.at[9])
    load_moves = pltpu.make_async_copy(moves_in, moves, load_sems.at[0])
    load_tails = pltpu.make_async_copy(tails_in, tails, load_sems.at[1])
    load_fresh = pltpu.make_async_copy(fresh_in, fresh_ref, load_sems.at[2])
    load_query = pltpu.make_async_copy(query_in, query_ref, load_sems.at[3])
    load_residual = pltpu.make_async_copy(residual_in, residual_ref, load_sems.at[4])
    load_cache = pltpu.make_async_copy(cache_in, cache, load_sems.at[5])
    load_proj = pltpu.make_async_copy(proj_in, proj, load_sems.at[6])
    load_moves.start()
    load_tails.start()
    load_fresh.start()
    load_lengths.start()
    load_prompts.start()
    lax.fori_loop(1, groups, greet, 0)
    pl.semaphore_signal(barrier, inc=1, device_id=(me, other), device_id_type=MESH)
    for step in range(1, chips):
        pl.semaphore_signal(
            barrier,
            inc=1,
            device_id=(me, chip_of(step) * CORES + core),
            device_id_type=MESH,
        )

    load_query.start()
    load_residual.start()
    load_cache.start()
    load_proj.start()
    load_moves.wait()
    find_slots(me, groups, branches_here, moves, slot_table, keep_rows)
    load_slots = pltpu.make_async_copy(slot_table, slot_scalars, load_sems.at[7])
    load_slots.start()
    load_slots.wait()
    load_tails.wait()
    load_fresh.wait()
    load_lengths.wait()
    load_prompts.wait()

    def pack(group, carry):
        for pick in range(2):
            branch = slot_scalars[group, pick]
            length = branch_length_ref[branch]
            for kind in range(2):
                staged[group * 2 + pick, kind] = written_rows(
                    tails[branch, kind], fresh_of(fresh_ref, branch, kind), length
                )
        return carry

    lax.fori_loop(0, groups, pack, 0)
    pl.semaphore_wait(barrier, groups - 1 + 1 + chips - 1)

    def tail_copy(step):
        return pltpu.make_async_remote_copy(
            src_ref=staged.at[pl.ds(peer_of(step) * 2, 2)],
            dst_ref=arrived_tails.at[pl.ds(me * 2, 2)],
            send_sem=tail_send_sems.at[step],
            recv_sem=tail_recv_sems.at[step],
            device_id=(peer_of(step), place),
            device_id_type=MESH,
        )

    def row_copy(step):
        return pltpu.make_async_remote_copy(
            src_ref=staged_rows.at[pl.ds(peer_of(step) * 2, 2)],
            dst_ref=arrived_rows.at[pl.ds(me * 2, 2)],
            send_sem=row_send_sems.at[step],
            recv_sem=row_recv_sems.at[step],
            device_id=(peer_of(step), place),
            device_id_type=MESH,
        )

    def pair_copy(chunk):
        return pltpu.make_async_remote_copy(
            src_ref=pair_send.at[chunk],
            dst_ref=pair_recv.at[chunk],
            send_sem=pair_send_sems.at[chunk],
            recv_sem=pair_recv_sems.at[chunk],
            device_id=(me, other),
            device_id_type=MESH,
        )

    def chip_copy(chunk, step):
        return pltpu.make_async_remote_copy(
            src_ref=chip_send.at[chunk, step - 1],
            dst_ref=chip_recv.at[chunk, step - 1],
            send_sem=chip_send_sems.at[chunk, step - 1],
            recv_sem=chip_recv_sems.at[chunk, step - 1],
            device_id=(me, chip_of(step) * CORES + core),
            device_id_type=MESH,
        )

    def send_tails(step, carry):
        tail_copy(step).start()
        return carry

    lax.fori_loop(1, groups, send_tails, 0)

    def widen(branch, carry):
        for i in range(new_count):
            both = fresh_ref[branch, i].astype(jnp.float32)
            for kind in range(2):
                fresh_wide[kind, i, pl.ds(branch, 1)] = both[kind : kind + 1]
        return carry

    lax.fori_loop(0, branches_here, widen, 0)
    spread(branch_length_ref, length_ref)
    spread(branch_prompt_ref, second_ref, me * cache.shape[0])
    load_query.wait()
    load_residual.wait()
    load_cache.wait()
    load_proj.wait()

    def project(chunk):
        first = pl.multiple_of(chunk * spans, spans)
        lhs = jnp.concatenate([heads[i, pl.ds(first, spans)] for i in range(new_count)], axis=0)
        for y in range(chips):
            column = pl.multiple_of((y * CORES + core) * width, width)
            own[chunk, y] = jnp.dot(
                lhs, proj[:, pl.ds(column, width)], preferred_element_type=jnp.float32
            )
            column = pl.multiple_of((y * CORES + CORES - 1 - core) * width, width)
            pair_send[chunk, y] = jnp.dot(
                lhs, proj[:, pl.ds(column, width)], preferred_element_type=jnp.float32
            ).astype(pair_send.dtype)
        pair_copy(chunk).start()

    def exchange(chunk):
        pair_copy(chunk).wait()
        for step in range(1, chips):
            y = chip_of(step)
            both = own[chunk, y] + pair_recv[chunk, y].astype(jnp.float32)
            chip_send[chunk, step - 1] = both.astype(chip_send.dtype)
            chip_copy(chunk, step).start()

    def finish(chunk):
        first = pl.multiple_of(chunk * spans, spans)
        summed = own[chunk, chip] + pair_recv[chunk, chip].astype(jnp.float32)
        for step in range(1, chips):
            chip_copy(chunk, step).wait()
            summed += chip_recv[chunk, step - 1].astype(jnp.float32)
        for i in range(new_count):
            rows = summed[i * spans : (i + 1) * spans]
            rows += residual_ref[i, pl.ds(first, spans)].astype(jnp.float32)
            keep = jnp.concatenate([keep_rows[pl.ds(first, spans)]] * (width // HEAD), axis=1) > 0
            mixed_out[i, pl.ds(first, spans)] = jnp.where(keep, rows, 0.0).astype(mixed_out.dtype)
            for at in range(0, width, HEAD):
                wide_rows[pl.ds(first, spans), i * (width // HEAD) + at // HEAD] = rows[
                    :, at : at + HEAD
                ]

    def work(chunk, carry):
        def tile(index, inner):
            first = pl.multiple_of((chunk * TILES + index) * GROUP, GROUP)
            attend_tile(
                first, query_ref, cache, tails, fresh_wide, length_ref, second_ref, heads, scores
            )
            return inner

        lax.fori_loop(0, TILES, tile, 0)

        @pl.when(chunk > 0)
        def _():
            exchange(chunk - 1)

        project(chunk)
        return carry

    lax.fori_loop(0, chunks, work, 0)
    exchange(chunks - 1)

    def settle(branch, carry):
        keep = jnp.broadcast_to(keep_rows[pl.ds(branch, 1)], tails.shape[2:]) > 0
        length = branch_length_ref[branch]
        for kind in range(2):
            rows = written_rows(tails[branch, kind], fresh_of(fresh_ref, branch, kind), length)
            rows = jnp.where(keep, rows.astype(jnp.float32), 0.0)
            tails_out[branch, kind] = rows.astype(tails_out.dtype)
        return carry

    def finish_chunk(chunk, carry):
        finish(chunk)
        return carry

    wide_rows[...] = jnp.zeros_like(wide_rows)
    lax.fori_loop(0, chunks, finish_chunk, 0)

    def pack_rows(group, carry):
        for pick in range(2):
            rows = wide_rows[slot_scalars[group, pick]]
            staged_rows[group * 2 + pick] = rows.astype(staged_rows.dtype)
        return carry

    lax.fori_loop(0, groups, pack_rows, 0)

    def send_rows(step, carry):
        row_copy(step).start()
        return carry

    lax.fori_loop(1, groups, send_rows, 0)
    lax.fori_loop(0, branches_here, settle, 0)
    for pick in range(2):
        arrived_tails[me * 2 + pick] = jnp.zeros(arrived_tails.shape[1:], arrived_tails.dtype)
        arrived_rows[me * 2 + pick] = jnp.zeros(arrived_rows.shape[1:], arrived_rows.dtype)

    def drain_sent(step, carry):
        tail_copy(step).wait_send()
        row_copy(step).wait_send()
        return carry

    def drain_rows(step, carry):
        row_copy(step).wait_recv()
        return carry

    def drain_tails(step, carry):
        tail_copy(step).wait_recv()
        return carry

    def place_row(row, carry):
        slot = slot_scalars[row, 2]
        value = arrived_rows[jnp.maximum(slot, 0)].astype(jnp.float32)
        value = jnp.where(slot >= 0, value, 0.0)
        for line in range(stage.shape[0]):
            stage[line, pl.ds(row, 1)] = value[line : line + 1]
        return carry

    def place_tail(row, carry):
        slot = slot_scalars[row, 2]
        at = jnp.maximum(slot, 0)
        for kind in range(2):
            value = arrived_tails[at, kind]
            value = jnp.where(slot >= 0, value, jnp.zeros_like(value))
            tails_out[branches_here + row, kind] = value
        return carry

    incoming = groups - 1
    lax.fori_loop(1, groups, drain_rows, 0)
    lax.fori_loop(0, incoming, place_row, 0)
    for i in range(new_count):
        for at in range(0, width, HEAD):
            line = i * (width // HEAD) + at // HEAD
            mixed_out[i, branches_here:, at : at + HEAD] = stage[line, :incoming].astype(
                mixed_out.dtype
            )
    lax.fori_loop(1, groups, drain_sent, 0)
    lax.fori_loop(1, groups, drain_tails, 0)
    lax.fori_loop(0, incoming, place_tail, 0)


def block(*arrays):
    lengths, prompt_of, moves, queries, residual, fresh, tails, cache, proj = arrays
    groups, chips = lax.axis_size("dp"), lax.axis_size("tensor") // CORES
    new_count, branches_here, width = queries.shape
    spans = GROUP * TILES
    chunks = branches_here // spans
    slots = branches_here + groups - 1
    rows = new_count * (width // HEAD) * GROUP
    kind = queries.dtype
    vmem = pl.BlockSpec(memory_space=pltpu.VMEM)
    hbm = pl.BlockSpec(memory_space=pl.ANY)
    flops = 8 * new_count * branches_here * (width // HEAD) * cache.shape[2] * HEAD
    dma = pltpu.SemaphoreType.DMA

    def body(*refs):
        block_kernel(groups, chips, *refs)

    return pl.pallas_call(
        body,
        out_shape=[
            pltpu.VMEM((new_count, slots, width), kind),
            pltpu.VMEM((slots,) + tails.shape[1:], kind),
        ],
        in_specs=[pl.BlockSpec(memory_space=pltpu.HBM)] * 9,
        out_specs=[vmem, vmem],
        scratch_shapes=[
            pltpu.VMEM((groups * 2, ROW, HEAD), kind),
            pltpu.VMEM((groups * 2,) + tails.shape[1:], kind),
            pltpu.VMEM((new_count * (width // HEAD), groups, HEAD), jnp.float32),
            pltpu.SMEM(lengths.shape, jnp.int32),
            pltpu.SMEM(prompt_of.shape, jnp.int32),
            pltpu.VMEM(moves.shape, jnp.int32),
            pltpu.VMEM((groups, HEAD), jnp.int32),
            pltpu.SMEM((groups, HEAD), jnp.int32),
            pltpu.VMEM((branches_here, HEAD), jnp.int32),
            pltpu.VMEM((branches_here, HEAD), jnp.int32),
            pltpu.VMEM((branches_here, HEAD), jnp.int32),
            pltpu.VMEM(queries.shape, kind),
            pltpu.VMEM(residual.shape, kind),
            pltpu.VMEM(fresh.shape, kind),
            pltpu.VMEM(tails.shape, kind),
            pltpu.VMEM(cache.shape, kind),
            pltpu.VMEM(proj.shape, kind),
            pltpu.VMEM((groups * 2,) + tails.shape[1:], kind),
            pltpu.VMEM((groups * 2, ROW, HEAD), kind),
            pltpu.VMEM((2, new_count, branches_here, HEAD), jnp.float32),
            pltpu.VMEM((rows, cache.shape[2]), jnp.float32),
            pltpu.VMEM(queries.shape, kind),
            pltpu.VMEM((chunks, chips, new_count * spans, width), jnp.float32),
            pltpu.VMEM((chunks, chips, new_count * spans, width), kind),
            pltpu.VMEM((chunks, chips, new_count * spans, width), kind),
            pltpu.VMEM((chunks, chips - 1, new_count * spans, width), kind),
            pltpu.VMEM((chunks, chips - 1, new_count * spans, width), kind),
            pltpu.VMEM((branches_here, ROW, HEAD), jnp.float32),
            dma((10,)),
            dma((groups,)),
            dma((groups,)),
            dma((groups,)),
            dma((groups,)),
            dma((chunks,)),
            dma((chunks,)),
            dma((chunks, chips - 1)),
            dma((chunks, chips - 1)),
        ],
        cost_estimate=pl.CostEstimate(
            flops=flops, bytes_accessed=20 * MIB, transcendentals=flops // 1024
        ),
        compiler_params=pltpu.CompilerParams(
            collective_id=0, has_side_effects=True, vmem_limit_bytes=46 * MIB
        ),
    )(*(pltpu.with_memory_space_constraint(array, pltpu.HBM) for array in arrays))


def store_kernel(mixed_in, tails_in, mixed_ref, tails_ref, sems):
    rows = tails_in.shape[0]
    share = -(-rows // PARTS)
    copies = [pltpu.make_async_copy(mixed_in, mixed_ref, sems.at[PARTS])]
    for part in range(PARTS):
        at = pl.ds(part * share, min(share, rows - part * share))
        copies.append(pltpu.make_async_copy(tails_in.at[at], tails_ref.at[at], sems.at[part]))
    for copy in copies:
        copy.start()
    for copy in copies:
        copy.wait()


def store(mixed, tails):
    hbm = pl.BlockSpec(memory_space=pl.ANY)
    return pl.pallas_call(
        store_kernel,
        out_shape=[jax.ShapeDtypeStruct(array.shape, array.dtype) for array in (mixed, tails)],
        in_specs=[hbm] * 2,
        out_specs=[hbm] * 2,
        scratch_shapes=[pltpu.SemaphoreType.DMA((PARTS + 1,))],
        compiler_params=pltpu.CompilerParams(vmem_limit_bytes=8 * MIB),
    )(mixed, tails)


def on_device(queries, prompt_cache, tails, fresh, residual, out_proj, lengths, prompt_of, moves):
    mixed, tails_out = block(
        lengths,
        prompt_of,
        jnp.transpose(moves),
        jnp.transpose(queries, (1, 0, 2)),
        jnp.transpose(residual, (1, 0, 2)),
        fresh,
        tails,
        prompt_cache,
        out_proj,
    )
    mixed, tails_out = store(mixed, tails_out)
    return (jnp.transpose(mixed, (1, 0, 2)), tails_out)


def solution(mesh):
    in_specs = (
        P("dp", None, "tensor"),
        P("dp", None, None, "tensor"),
        P("dp", None, None, "tensor"),
        P("dp", None, None, "tensor"),
        P("dp", None, "tensor"),
        P("tensor", None),
        P("dp"),
        P("dp"),
        P(),
    )
    out_specs = (P("dp", None, "tensor"), P("dp", None, None, "tensor"))
    return jax.shard_map(
        on_device, mesh=mesh, in_specs=in_specs, out_specs=out_specs, check_vma=False
    )
```

```python
import math

import jax
import jax.numpy as jnp
from jax import lax
from jax.experimental import pallas as pl
from jax.experimental.pallas import tpu as pltpu
from jax.sharding import PartitionSpec as P

HEAD = 128
GROUP = 16
TILES = 2
CHUNK = 512
CORES = 2
ROW = 16
MIB = 1 << 20
PARTS = 4
MESH = pl.DeviceIdType.MESH


def wrapped(index, size):
    return jnp.where(index >= size, index - size, index)


def written_rows(rows, fresh, length):
    at = lax.broadcasted_iota(jnp.int32, rows.shape, 0)
    wide = rows.astype(jnp.float32)
    for i, line in enumerate(fresh):
        wide = jnp.where(at == length + i, line, wide)
    return wide.astype(rows.dtype)


def fresh_of(fresh_ref, branch, kind):
    pairs = [fresh_ref[branch, i].astype(jnp.float32) for i in range(fresh_ref.shape[1])]
    return [pair[kind : kind + 1] for pair in pairs]


def attend_tile(first, query_ref, cache, tails, fresh_wide, length_ref, second_ref, heads, scores):
    new_count = query_ref.shape[0]
    share = query_ref.shape[2] // HEAD
    keys = cache.shape[2]
    tail_rows = tails.shape[2]
    tail_keys = GROUP * tail_rows
    blocks = new_count * share
    rows = blocks * GROUP
    factor = math.log2(math.e) / math.sqrt(HEAD)
    contract_last = (((1,), (1,)), ((), ()))

    def lanes(op, value, carry):
        for at in range(0, value.shape[1], HEAD):
            carry = op(carry, value[:, at : at + HEAD])
        return carry

    def fresh_block(kind):
        parts = [fresh_wide[kind, i, pl.ds(first, GROUP)] for i in range(new_count)]
        parts.append(jnp.zeros((HEAD - new_count * GROUP, HEAD), jnp.float32))
        return jnp.concatenate(parts, axis=0).astype(jnp.bfloat16)

    query = jnp.concatenate(
        [
            query_ref[i, pl.ds(first, GROUP), h * HEAD : (h + 1) * HEAD]
            for i in range(new_count)
            for h in range(share)
        ],
        axis=0,
    )
    second = jnp.concatenate([second_ref[pl.ds(first, GROUP)]] * blocks, axis=0) > 0
    nothing = jnp.zeros_like(query)
    both = jnp.concatenate(
        [jnp.where(second, nothing, query), jnp.where(second, query, nothing)], axis=1
    )
    top = jnp.full((rows, HEAD), -jnp.inf, jnp.float32)
    for at in range(0, keys, CHUNK):
        key_block = jnp.concatenate(
            [cache[0, 0, at : at + CHUNK], cache[1, 0, at : at + CHUNK]], axis=1
        )
        block = lax.dot_general(both, key_block, contract_last, preferred_element_type=jnp.float32)
        scores[:, at : at + CHUNK] = block
        top = lanes(jnp.maximum, block, top)
    tail_scores = lax.dot_general(
        query,
        tails[pl.ds(first, GROUP), 0].reshape(tail_keys, HEAD),
        contract_last,
        preferred_element_type=jnp.float32,
    )
    length = jnp.concatenate([length_ref[pl.ds(first, GROUP)]] * blocks, axis=0)
    row_at = lax.broadcasted_iota(jnp.int32, (rows, HEAD), 0)
    key_at = lax.broadcasted_iota(jnp.int32, (rows, HEAD), 1)
    held = []
    for at in range(0, tail_keys, HEAD):
        seen = (row_at % GROUP == (key_at + at) // tail_rows) & (key_at % tail_rows < length)
        held.append(jnp.where(seen, tail_scores[:, at : at + HEAD], -jnp.inf))
    tail_scores = jnp.concatenate(held, axis=1)
    fresh_scores = lax.dot_general(
        query, fresh_block(0), contract_last, preferred_element_type=jnp.float32
    )
    seen = (row_at % GROUP == key_at % GROUP) & (key_at // GROUP <= row_at // (GROUP * share))
    fresh_scores = jnp.where(seen, fresh_scores, -jnp.inf)
    top = jnp.maximum(lanes(jnp.maximum, tail_scores, top), fresh_scores)
    top = jnp.max(top, axis=1, keepdims=True)
    total = jnp.zeros((rows, HEAD), jnp.float32)
    pair = jnp.zeros((rows, 2 * HEAD), jnp.float32)
    for at in range(0, keys, CHUNK):
        expo = jnp.exp2((scores[:, at : at + CHUNK] - top) * factor)
        total = lanes(jnp.add, expo, total)
        value_block = jnp.concatenate(
            [cache[0, 1, at : at + CHUNK], cache[1, 1, at : at + CHUNK]], axis=1
        )
        pair += jnp.dot(expo.astype(jnp.bfloat16), value_block, preferred_element_type=jnp.float32)
    mixed = jnp.where(second, pair[:, HEAD:], pair[:, :HEAD])
    expo = jnp.exp2((tail_scores - top) * factor)
    total = lanes(jnp.add, expo, total)
    mixed += jnp.dot(
        expo.astype(jnp.bfloat16),
        tails[pl.ds(first, GROUP), 1].reshape(tail_keys, HEAD),
        preferred_element_type=jnp.float32,
    )
    expo = jnp.exp2((fresh_scores - top) * factor)
    total += expo
    mixed += jnp.dot(
        expo.astype(jnp.bfloat16), fresh_block(1), preferred_element_type=jnp.float32
    )
    result = (mixed / jnp.sum(total, axis=1, keepdims=True)).astype(heads.dtype)
    for i in range(new_count):
        for h in range(share):
            at = (i * share + h) * GROUP
            heads[i, pl.ds(first, GROUP), h * HEAD : (h + 1) * HEAD] = result[at : at + GROUP]


def find_departures(me, groups, branches_here, moves, slot_table):
    branch, source, target = (moves[at : at + 1] for at in range(3))
    entries = moves.shape[1]
    group = lax.broadcasted_iota(jnp.int32, (groups, entries), 0)
    entry = lax.broadcasted_iota(jnp.int32, (groups, entries), 1)
    local = branch - me * branches_here
    far = entries * HEAD
    code = jnp.where((source == me) & (target == group), entry * HEAD + local, -1)
    last = jnp.max(code, axis=1, keepdims=True)
    first = jnp.min(jnp.where(code >= 0, code, far), axis=1, keepdims=True)
    first = jnp.where(first < far, first % HEAD, 0)
    last = jnp.where(last >= 0, last % HEAD, 0)
    column = lax.broadcasted_iota(jnp.int32, slot_table.shape, 1)
    slot_table[...] = jnp.where(column == 0, first, last)


def find_arrivals(me, groups, branches_here, moves, slot_table, keep_rows):
    branch, source, target = (moves[at : at + 1] for at in range(3))
    entries = moves.shape[1]
    group = lax.broadcasted_iota(jnp.int32, (groups, entries), 0)
    entry = lax.broadcasted_iota(jnp.int32, (groups, entries), 1)
    here = target == me
    code = jnp.where(here & (source == group), entry, -1)
    last = jnp.max(code, axis=1, keepdims=True)
    first = jnp.min(jnp.where(code >= 0, code, entries), axis=1, keepdims=True)

    def arrival(at):
        return jnp.sum(jnp.where(here & (entry < at), 1, 0), axis=1, keepdims=True)

    square = (groups, groups)
    row = lax.broadcasted_iota(jnp.int32, square, 0)
    column = lax.broadcasted_iota(jnp.int32, square, 1)

    def flat(value):
        return jnp.sum(jnp.where(row == column, value, 0), axis=0, keepdims=True)

    once = flat(jnp.where(last >= 0, arrival(first), -1))
    twice = flat(jnp.where(last > first, arrival(last), -1))
    slot = jnp.where(once == row, column * 2, jnp.where(twice == row, column * 2 + 1, -1))
    slot = jnp.max(slot, axis=1, keepdims=True)
    column = lax.broadcasted_iota(jnp.int32, slot_table.shape, 1)
    slot_table[...] = jnp.where(column == 2, slot, slot_table[...])
    row = lax.broadcasted_iota(jnp.int32, (branches_here, entries), 0)
    gone = jnp.where((source == me) & (branch - me * branches_here == row), 1, 0)
    gone = jnp.max(gone, axis=1, keepdims=True)
    keep_rows[...] = jnp.broadcast_to(1 - gone, keep_rows.shape)


def spread(scalars, rows, base=0):
    def step(at, carry):
        rows[pl.ds(at, 1)] = jnp.full((1, rows.shape[1]), scalars[at] - base, jnp.int32)
        return carry

    lax.fori_loop(0, rows.shape[0], step, 0)


def block_kernel(
    groups,
    chips,
    lengths_in,
    prompt_of_in,
    moves_in,
    query_in,
    residual_in,
    fresh_in,
    tails_in,
    cache_in,
    proj_in,
    mixed_out,
    tails_out,
    arrived_rows,
    arrived_tails,
    stage,
    branch_length_ref,
    branch_prompt_ref,
    moves,
    slot_table,
    slot_scalars,
    keep_rows,
    length_ref,
    second_ref,
    query_ref,
    residual_ref,
    fresh_ref,
    tails,
    cache,
    proj,
    staged,
    staged_rows,
    fresh_wide,
    scores,
    heads,
    own,
    pair_send,
    pair_recv,
    chip_send,
    chip_recv,
    wide_rows,
    load_sems,
    tail_send_sems,
    tail_recv_sems,
    row_send_sems,
    row_recv_sems,
    pair_send_sems,
    pair_recv_sems,
    chip_send_sems,
    chip_recv_sems,
):
    new_count, branches_here, width = query_ref.shape
    me = lax.axis_index("dp")
    place = lax.axis_index("tensor")
    chip, core = place // CORES, place % CORES
    other = chip * CORES + (CORES - 1 - core)
    spans = GROUP * TILES
    chunks = branches_here // spans

    def peer_of(step):
        return wrapped(me + step, groups)

    def chip_of(step):
        return wrapped(chip + step, chips)

    barrier = pltpu.get_barrier_semaphore()

    def greet(step, carry):
        pl.semaphore_signal(
            barrier, inc=1, device_id=(peer_of(step), place), device_id_type=MESH
        )
        return carry

    load_lengths = pltpu.make_async_copy(lengths_in, branch_length_ref, load_sems.at[8])
    load_prompts = pltpu.make_async_copy(prompt_of_in, branch_prompt_ref, load_sems.at[9])
    load_moves = pltpu.make_async_copy(moves_in, moves, load_sems.at[0])
    load_tails = pltpu.make_async_copy(tails_in, tails, load_sems.at[1])
    load_fresh = pltpu.make_async_copy(fresh_in, fresh_ref, load_sems.at[2])
    load_query = pltpu.make_async_copy(query_in, query_ref, load_sems.at[3])
    load_residual = pltpu.make_async_copy(residual_in, residual_ref, load_sems.at[4])
    load_cache = pltpu.make_async_copy(cache_in, cache, load_sems.at[5])
    load_proj = pltpu.make_async_copy(proj_in, proj, load_sems.at[6])
    load_moves.start()
    load_tails.start()
    load_fresh.start()
    load_lengths.start()
    load_prompts.start()
    lax.fori_loop(1, groups, greet, 0)
    pl.semaphore_signal(barrier, inc=1, device_id=(me, other), device_id_type=MESH)
    for step in range(1, chips):
        pl.semaphore_signal(
            barrier,
            inc=1,
            device_id=(me, chip_of(step) * CORES + core),
            device_id_type=MESH,
        )

    load_query.start()
    load_residual.start()
    load_cache.start()
    load_proj.start()
    load_moves.wait()
    find_departures(me, groups, branches_here, moves, slot_table)
    load_slots = pltpu.make_async_copy(slot_table, slot_scalars, load_sems.at[7])
    load_slots.start()
    load_slots.wait()
    load_tails.wait()
    load_fresh.wait()
    load_lengths.wait()
    load_prompts.wait()

    def pack(step, carry):
        group = peer_of(step)
        for pick in range(2):
            branch = slot_scalars[group, pick]
            length = branch_length_ref[branch]
            for kind in range(2):
                staged[group * 2 + pick, kind] = written_rows(
                    tails[branch, kind], fresh_of(fresh_ref, branch, kind), length
                )
        tail_copy(step).start()
        return carry

    pl.semaphore_wait(barrier, groups - 1 + 1 + chips - 1)

    def tail_copy(step):
        return pltpu.make_async_remote_copy(
            src_ref=staged.at[pl.ds(peer_of(step) * 2, 2)],
            dst_ref=arrived_tails.at[pl.ds(me * 2, 2)],
            send_sem=tail_send_sems.at[step],
            recv_sem=tail_recv_sems.at[step],
            device_id=(peer_of(step), place),
            device_id_type=MESH,
        )

    def row_copy(step):
        return pltpu.make_async_remote_copy(
            src_ref=staged_rows.at[pl.ds(peer_of(step) * 2, 2)],
            dst_ref=arrived_rows.at[pl.ds(me * 2, 2)],
            send_sem=row_send_sems.at[step],
            recv_sem=row_recv_sems.at[step],
            device_id=(peer_of(step), place),
            device_id_type=MESH,
        )

    def pair_copy(chunk):
        return pltpu.make_async_remote_copy(
            src_ref=pair_send.at[chunk],
            dst_ref=pair_recv.at[chunk],
            send_sem=pair_send_sems.at[chunk],
            recv_sem=pair_recv_sems.at[chunk],
            device_id=(me, other),
            device_id_type=MESH,
        )

    def chip_copy(chunk, step):
        return pltpu.make_async_remote_copy(
            src_ref=chip_send.at[chunk, step - 1],
            dst_ref=chip_recv.at[chunk, step - 1],
            send_sem=chip_send_sems.at[chunk, step - 1],
            recv_sem=chip_recv_sems.at[chunk, step - 1],
            device_id=(me, chip_of(step) * CORES + core),
            device_id_type=MESH,
        )

    lax.fori_loop(1, groups, pack, 0)
    find_arrivals(me, groups, branches_here, moves, slot_table, keep_rows)
    load_slots.start()
    load_slots.wait()

    def widen(branch, carry):
        for i in range(new_count):
            both = fresh_ref[branch, i].astype(jnp.float32)
            for kind in range(2):
                fresh_wide[kind, i, pl.ds(branch, 1)] = both[kind : kind + 1]
        return carry

    lax.fori_loop(0, branches_here, widen, 0)
    spread(branch_length_ref, length_ref)
    spread(branch_prompt_ref, second_ref, me * cache.shape[0])
    load_query.wait()
    load_residual.wait()
    load_cache.wait()
    load_proj.wait()

    def project(chunk):
        first = pl.multiple_of(chunk * spans, spans)
        lhs = jnp.concatenate([heads[i, pl.ds(first, spans)] for i in range(new_count)], axis=0)
        for y in range(chips):
            column = pl.multiple_of((y * CORES + core) * width, width)
            own[chunk, y] = jnp.dot(
                lhs, proj[:, pl.ds(column, width)], preferred_element_type=jnp.float32
            )
            column = pl.multiple_of((y * CORES + CORES - 1 - core) * width, width)
            pair_send[chunk, y] = jnp.dot(
                lhs, proj[:, pl.ds(column, width)], preferred_element_type=jnp.float32
            ).astype(pair_send.dtype)
        pair_copy(chunk).start()

    def exchange(chunk):
        pair_copy(chunk).wait()
        for step in range(1, chips):
            y = chip_of(step)
            both = own[chunk, y] + pair_recv[chunk, y].astype(jnp.float32)
            chip_send[chunk, step - 1] = both.astype(chip_send.dtype)
            chip_copy(chunk, step).start()

    def finish(chunk):
        first = pl.multiple_of(chunk * spans, spans)
        summed = own[chunk, chip] + pair_recv[chunk, chip].astype(jnp.float32)
        for step in range(1, chips):
            chip_copy(chunk, step).wait()
            summed += chip_recv[chunk, step - 1].astype(jnp.float32)
        for i in range(new_count):
            rows = summed[i * spans : (i + 1) * spans]
            rows += residual_ref[i, pl.ds(first, spans)].astype(jnp.float32)
            keep = jnp.concatenate([keep_rows[pl.ds(first, spans)]] * (width // HEAD), axis=1) > 0
            mixed_out[i, pl.ds(first, spans)] = jnp.where(keep, rows, 0.0).astype(mixed_out.dtype)
            for at in range(0, width, HEAD):
                wide_rows[pl.ds(first, spans), i * (width // HEAD) + at // HEAD] = rows[
                    :, at : at + HEAD
                ]

    def work(chunk, carry):
        def tile(index, inner):
            first = pl.multiple_of((chunk * TILES + index) * GROUP, GROUP)
            attend_tile(
                first, query_ref, cache, tails, fresh_wide, length_ref, second_ref, heads, scores
            )
            return inner

        lax.fori_loop(0, TILES, tile, 0)

        @pl.when(chunk > 0)
        def _():
            exchange(chunk - 1)

        project(chunk)
        return carry

    lax.fori_loop(0, chunks, work, 0)
    exchange(chunks - 1)

    def settle(branch, carry):
        keep = jnp.broadcast_to(keep_rows[pl.ds(branch, 1)], tails.shape[2:]) > 0
        length = branch_length_ref[branch]
        for kind in range(2):
            rows = written_rows(tails[branch, kind], fresh_of(fresh_ref, branch, kind), length)
            rows = jnp.where(keep, rows.astype(jnp.float32), 0.0)
            tails_out[branch, kind] = rows.astype(tails_out.dtype)
        return carry

    def finish_chunk(chunk, carry):
        finish(chunk)
        return carry

    wide_rows[...] = jnp.zeros_like(wide_rows)
    lax.fori_loop(0, chunks, finish_chunk, 0)

    def pack_rows(group, carry):
        for pick in range(2):
            rows = wide_rows[slot_scalars[group, pick]]
            staged_rows[group * 2 + pick] = rows.astype(staged_rows.dtype)
        return carry

    lax.fori_loop(0, groups, pack_rows, 0)

    def send_rows(step, carry):
        row_copy(step).start()
        return carry

    lax.fori_loop(1, groups, send_rows, 0)
    lax.fori_loop(0, branches_here, settle, 0)
    for pick in range(2):
        arrived_tails[me * 2 + pick] = jnp.zeros(arrived_tails.shape[1:], arrived_tails.dtype)
        arrived_rows[me * 2 + pick] = jnp.zeros(arrived_rows.shape[1:], arrived_rows.dtype)

    def drain_sent(step, carry):
        tail_copy(step).wait_send()
        row_copy(step).wait_send()
        return carry

    def drain_rows(step, carry):
        row_copy(step).wait_recv()
        return carry

    def drain_tails(step, carry):
        tail_copy(step).wait_recv()
        return carry

    def place_row(row, carry):
        slot = slot_scalars[row, 2]
        value = arrived_rows[jnp.maximum(slot, 0)].astype(jnp.float32)
        value = jnp.where(slot >= 0, value, 0.0)
        for line in range(stage.shape[0]):
            stage[line, pl.ds(row, 1)] = value[line : line + 1]
        return carry

    def place_tail(row, carry):
        slot = slot_scalars[row, 2]
        at = jnp.maximum(slot, 0)
        for kind in range(2):
            value = arrived_tails[at, kind]
            value = jnp.where(slot >= 0, value, jnp.zeros_like(value))
            tails_out[branches_here + row, kind] = value
        return carry

    incoming = groups - 1
    lax.fori_loop(1, groups, drain_tails, 0)
    lax.fori_loop(0, incoming, place_tail, 0)
    lax.fori_loop(1, groups, drain_rows, 0)
    lax.fori_loop(0, incoming, place_row, 0)
    for i in range(new_count):
        for at in range(0, width, HEAD):
            line = i * (width // HEAD) + at // HEAD
            mixed_out[i, branches_here:, at : at + HEAD] = stage[line, :incoming].astype(
                mixed_out.dtype
            )
    lax.fori_loop(1, groups, drain_sent, 0)


def block(*arrays):
    lengths, prompt_of, moves, queries, residual, fresh, tails, cache, proj = arrays
    groups, chips = lax.axis_size("dp"), lax.axis_size("tensor") // CORES
    new_count, branches_here, width = queries.shape
    spans = GROUP * TILES
    chunks = branches_here // spans
    slots = branches_here + groups - 1
    rows = new_count * (width // HEAD) * GROUP
    kind = queries.dtype
    vmem = pl.BlockSpec(memory_space=pltpu.VMEM)
    hbm = pl.BlockSpec(memory_space=pl.ANY)
    flops = 8 * new_count * branches_here * (width // HEAD) * cache.shape[2] * HEAD
    dma = pltpu.SemaphoreType.DMA

    def body(*refs):
        block_kernel(groups, chips, *refs)

    return pl.pallas_call(
        body,
        out_shape=[
            pltpu.VMEM((new_count, slots, width), kind),
            pltpu.VMEM((slots,) + tails.shape[1:], kind),
        ],
        in_specs=[pl.BlockSpec(memory_space=pltpu.HBM)] * 9,
        out_specs=[vmem, vmem],
        scratch_shapes=[
            pltpu.VMEM((groups * 2, ROW, HEAD), kind),
            pltpu.VMEM((groups * 2,) + tails.shape[1:], kind),
            pltpu.VMEM((new_count * (width // HEAD), groups, HEAD), jnp.float32),
            pltpu.SMEM(lengths.shape, jnp.int32),
            pltpu.SMEM(prompt_of.shape, jnp.int32),
            pltpu.VMEM(moves.shape, jnp.int32),
            pltpu.VMEM((groups, HEAD), jnp.int32),
            pltpu.SMEM((groups, HEAD), jnp.int32),
            pltpu.VMEM((branches_here, HEAD), jnp.int32),
            pltpu.VMEM((branches_here, HEAD), jnp.int32),
            pltpu.VMEM((branches_here, HEAD), jnp.int32),
            pltpu.VMEM(queries.shape, kind),
            pltpu.VMEM(residual.shape, kind),
            pltpu.VMEM(fresh.shape, kind),
            pltpu.VMEM(tails.shape, kind),
            pltpu.VMEM(cache.shape, kind),
            pltpu.VMEM(proj.shape, kind),
            pltpu.VMEM((groups * 2,) + tails.shape[1:], kind),
            pltpu.VMEM((groups * 2, ROW, HEAD), kind),
            pltpu.VMEM((2, new_count, branches_here, HEAD), jnp.float32),
            pltpu.VMEM((rows, cache.shape[2]), jnp.float32),
            pltpu.VMEM(queries.shape, kind),
            pltpu.VMEM((chunks, chips, new_count * spans, width), jnp.float32),
            pltpu.VMEM((chunks, chips, new_count * spans, width), kind),
            pltpu.VMEM((chunks, chips, new_count * spans, width), kind),
            pltpu.VMEM((chunks, chips - 1, new_count * spans, width), kind),
            pltpu.VMEM((chunks, chips - 1, new_count * spans, width), kind),
            pltpu.VMEM((branches_here, ROW, HEAD), jnp.float32),
            dma((10,)),
            dma((groups,)),
            dma((groups,)),
            dma((groups,)),
            dma((groups,)),
            dma((chunks,)),
            dma((chunks,)),
            dma((chunks, chips - 1)),
            dma((chunks, chips - 1)),
        ],
        cost_estimate=pl.CostEstimate(
            flops=flops, bytes_accessed=20 * MIB, transcendentals=flops // 1024
        ),
        compiler_params=pltpu.CompilerParams(
            collective_id=0, has_side_effects=True, vmem_limit_bytes=46 * MIB
        ),
    )(*(pltpu.with_memory_space_constraint(array, pltpu.HBM) for array in arrays))


def store_kernel(mixed_in, tails_in, mixed_ref, tails_ref, sems):
    rows = tails_in.shape[0]
    share = -(-rows // PARTS)
    copies = [pltpu.make_async_copy(mixed_in, mixed_ref, sems.at[PARTS])]
    for part in range(PARTS):
        at = pl.ds(part * share, min(share, rows - part * share))
        copies.append(pltpu.make_async_copy(tails_in.at[at], tails_ref.at[at], sems.at[part]))
    for copy in copies:
        copy.start()
    for copy in copies:
        copy.wait()


def store(mixed, tails):
    hbm = pl.BlockSpec(memory_space=pl.ANY)
    return pl.pallas_call(
        store_kernel,
        out_shape=[jax.ShapeDtypeStruct(array.shape, array.dtype) for array in (mixed, tails)],
        in_specs=[hbm] * 2,
        out_specs=[hbm] * 2,
        scratch_shapes=[pltpu.SemaphoreType.DMA((PARTS + 1,))],
        compiler_params=pltpu.CompilerParams(vmem_limit_bytes=8 * MIB),
    )(mixed, tails)


def on_device(queries, prompt_cache, tails, fresh, residual, out_proj, lengths, prompt_of, moves):
    mixed, tails_out = block(
        lengths,
        prompt_of,
        jnp.transpose(moves),
        jnp.transpose(queries, (1, 0, 2)),
        jnp.transpose(residual, (1, 0, 2)),
        fresh,
        tails,
        prompt_cache,
        out_proj,
    )
    mixed, tails_out = store(mixed, tails_out)
    return (jnp.transpose(mixed, (1, 0, 2)), tails_out)


def solution(mesh):
    in_specs = (
        P("dp", None, "tensor"),
        P("dp", None, None, "tensor"),
        P("dp", None, None, "tensor"),
        P("dp", None, None, "tensor"),
        P("dp", None, "tensor"),
        P("tensor", None),
        P("dp"),
        P("dp"),
        P(),
    )
    out_specs = (P("dp", None, "tensor"), P("dp", None, None, "tensor"))
    return jax.shard_map(
        on_device, mesh=mesh, in_specs=in_specs, out_specs=out_specs, check_vma=False
    )
```
